256 devices in a mesh: seq: 64 (over z, x, core), ffn: 4 (over y).
Axes of the slice: x: 4, y: 4, z: 8, core: 2. Of those that a mesh axis runs over, the one named last changes fastest.
Arguments:
- tokens: bfloat16 [64, 256, 8192], P('seq', None, 'ffn'), may hold values from -6 to 6
- cotangent: bfloat16 [64, 256, 8192], P('seq', None, 'ffn'), may hold values from -6 to 6
- block_masks: int32 [64, 128], replicated, may hold values from 0 to 1, as said below
- w_up: bfloat16 [8192, 16384], P('ffn', 'seq'), may hold values from -0.0625 to 0.0625
- w_gate: bfloat16 [8192, 16384], P('ffn', 'seq'), may hold values from -0.0625 to 0.0625
- w_down: bfloat16 [16384, 8192], P('seq', 'ffn'), may hold values from -0.25 to 0.25
Outputs:
- outputs: bfloat16 [64, 256, 8192], P('seq', None, 'ffn')
- grad_tokens: bfloat16 [64, 256, 8192], P('seq', None, 'ffn')
- grad_up: bfloat16 [8192, 16384], P('ffn', 'seq')
- grad_gate: bfloat16 [8192, 16384], P('ffn', 'seq')
- grad_down: bfloat16 [16384, 8192], P('seq', 'ffn')
The draws below stay inside these ranges and needn't reach their ends.
Inputs may be any that keep to these rules, and one draw needn't show every extreme that they name: `block_masks`: split the 128 blocks into runs of 2 consecutive blocks (owners). For every owner, between 1 and 3 groups have any block of that owner active, and some owner has exactly 3.
All inputs are finite; a program needn't handle non-finite values.
Results may differ from the reference program's by a relative error of at most 0.005.
Values may be sent and summed in bfloat16 or wider, within the bound.
A program may use at most 128 MiB of HBM per device.

```python
import jax
import jax.numpy as jnp
from jax import lax

D = 8192
FF = 16384
BLK = 128
GSIZE = 256
CAP = 3
GROUPS = 64
NB = 128
OWN_BLK = 2


def draw_block_masks(key, part):
    key = jax.random.fold_in(key, 11)
    owners = NB // OWN_BLK
    key_fullest, key_crowded, key_count, key_ranking, key_forced, key_extras = jax.random.split(key, 6)
    crowded = jax.random.randint(key_crowded, (owners,), 0, 2)
    added_count = jax.random.randint(key_count, (owners,), 0, CAP)
    counts = 1 + crowded * added_count
    fullest = jax.random.randint(key_fullest, (), 0, owners)
    counts = jnp.where(jnp.arange(owners) == fullest, CAP, counts)
    rank_keys = jax.random.split(key_ranking, owners)
    ranking = jax.vmap(lambda rank_key: jax.random.permutation(rank_key, GROUPS))(rank_keys)
    chosen = ranking < counts[:, None]
    forced = jax.random.randint(key_forced, (GROUPS, owners), 0, OWN_BLK)
    extras = jax.random.randint(key_extras, (GROUPS, owners, OWN_BLK), 0, 2)
    columns = jnp.arange(OWN_BLK)
    enabled = extras + (columns[None, None, :] == forced[:, :, None]).astype(jnp.int32) > 0
    result = (enabled & chosen.T[:, :, None]).astype(jnp.int32)
    return result.reshape(GROUPS, NB)


def levels(key, dims, shards, least, high):
    level, own = 1.0, jax.random.fold_in(key, 6)
    for dim, parts in shards:
        draws = jnp.exp(jax.random.uniform(jax.random.fold_in(own, dim), (parts,), jnp.float32, least / len(shards), high / len(shards)))
        level = level * jnp.repeat(draws, dims[dim] // parts).reshape([-1 if axis == dim else 1 for axis in range(len(dims))])
    return level


def normal_values(key, shape, spread, reach, pieces=(), held_as=jnp.bfloat16):
    values = jax.random.normal(key, shape, jnp.float32) * spread
    if len(pieces) > 0:
        values = levels(key, shape, pieces, -0.22, 0.18) * values
    return jnp.clip(values, min=-reach, max=reach).astype(held_as)


def setup_inputs(seed: int = 0) -> dict:
    key_list = jax.random.split(jax.random.key(seed), 7)
    tokens = normal_values(key_list[0], (GROUPS, GSIZE, D), 1.0, 6.0, ((0, 64), (2, 4)))
    cotangent = normal_values(key_list[1], (GROUPS, GSIZE, D), 1.0, 6.0, ((0, 64), (2, 4)))
    block_masks = draw_block_masks(jax.random.fold_in(key_list[6], 71), 0)
    w_up = normal_values(key_list[3], (D, FF), D ** -0.5, 0.0625, ((0, 4), (1, 64)))
    w_gate = normal_values(key_list[4], (D, FF), D ** -0.5, 0.0625, ((0, 4), (1, 64)))
    w_down = normal_values(key_list[5], (FF, D), (4 * BLK) ** -0.5, 0.25, ((0, 64), (1, 4)))
    return dict(tokens=tokens, cotangent=cotangent, block_masks=block_masks, w_up=w_up, w_gate=w_gate, w_down=w_down)


def reference(tokens, cotangent, block_masks, w_up, w_gate, w_down):
    grouped = tokens
    grouped_cot = cotangent
    row_count = CAP * GSIZE
    group_ids = jnp.arange(GROUPS, dtype=jnp.int32)
    slot_ids = jnp.arange(CAP, dtype=jnp.int32)
    grad_scale = 1.0 / GSIZE

    def block_step(totals, block_id):
        out_total, input_total = totals
        column = lax.dynamic_index_in_dim(block_masks, block_id, 1, keepdims=False)
        active = (column > 0).astype(jnp.int32)
        ordinal = jnp.cumsum(active) - 1
        picked = ((ordinal[None, :] == slot_ids[:, None]) & (active[None, :] > 0)).astype(jnp.int32)
        slot_group = jnp.sum(picked * group_ids[None, :], axis=1).astype(jnp.int32)
        occupied = jnp.sum(picked, axis=1).astype(jnp.float32)
        offset = (block_id * BLK).astype(jnp.int32)
        up_cols = lax.dynamic_slice_in_dim(w_up, offset, BLK, 1)
        gate_cols = lax.dynamic_slice_in_dim(w_gate, offset, BLK, 1)
        down_rows = lax.dynamic_slice_in_dim(w_down, offset, BLK, 0)
        token_rows = jnp.take(grouped, slot_group, axis=0).reshape(row_count, D)
        cotan_rows = jnp.take(grouped_cot, slot_group, axis=0).reshape(row_count, D)
        keep_rows = jnp.repeat(occupied, GSIZE)[:, None]
        up_pre = jnp.dot(token_rows, up_cols, preferred_element_type=jnp.float32)
        gate_pre = jnp.dot(token_rows, gate_cols, preferred_element_type=jnp.float32)
        rectified = jnp.maximum(gate_pre, jnp.float32(0.0))
        hidden = (rectified * rectified * up_pre * keep_rows).astype(jnp.bfloat16)
        out_part = jnp.dot(hidden, down_rows, preferred_element_type=jnp.float32).reshape(CAP, GSIZE, D)
        hidden_grad = jnp.dot(cotan_rows, down_rows.T, preferred_element_type=jnp.float32) * keep_rows
        up_grad = (hidden_grad * rectified * rectified).astype(jnp.bfloat16)
        gate_grad = (hidden_grad * up_pre * 2.0 * rectified).astype(jnp.bfloat16)
        input_part = jnp.dot(up_grad, up_cols.T, preferred_element_type=jnp.float32)
        input_part = input_part + jnp.dot(gate_grad, gate_cols.T, preferred_element_type=jnp.float32)
        input_part = input_part.reshape(CAP, GSIZE, D)
        up_block = (jnp.dot(token_rows.T, up_grad, preferred_element_type=jnp.float32) * grad_scale).astype(jnp.bfloat16)
        gate_block = (jnp.dot(token_rows.T, gate_grad, preferred_element_type=jnp.float32) * grad_scale).astype(jnp.bfloat16)
        down_block = (jnp.dot(hidden.T, cotan_rows, preferred_element_type=jnp.float32) * grad_scale).astype(jnp.bfloat16)
        out_total = out_total.at[slot_group].add(out_part)
        input_total = input_total.at[slot_group].add(input_part)
        return (out_total, input_total), (up_block, gate_block, down_block)

    start_totals = (jnp.zeros((GROUPS, GSIZE, D), jnp.float32), jnp.zeros((GROUPS, GSIZE, D), jnp.float32))
    totals, stacked = lax.scan(block_step, start_totals, jnp.arange(NB, dtype=jnp.int32))
    out_total, input_total = totals
    up_blocks, gate_blocks, down_blocks = stacked
    outputs = out_total.astype(jnp.bfloat16)
    grad_tokens = input_total.astype(jnp.bfloat16)
    grad_up = jnp.transpose(up_blocks, (1, 0, 2)).reshape(D, FF)
    grad_gate = jnp.transpose(gate_blocks, (1, 0, 2)).reshape(D, FF)
    grad_down = down_blocks.reshape(FF, D)
    return (outputs, grad_tokens, grad_up, grad_gate, grad_down)
```

```python
import functools

import jax
import jax.numpy as jnp
from jax import lax
from jax.experimental import pallas as pl
from jax.experimental.pallas import tpu as pltpu
from jax.sharding import PartitionSpec as P

BLK = 128
CAP = 3
PLANE = 8
ROWS = 16
CHUNKS = 2
MESH = pl.DeviceIdType.MESH
F32, BF16 = jnp.float32, jnp.bfloat16


def dot(left, right, dims):
    return lax.dot_general(left, right, (((dims[0],), (dims[1],)), ((), ())), preferred_element_type=F32)


def kernel(Z, S, Y, W, U, slots, column_group, row_mask, tok, cot, wu_in, wg_in, wd_in,
           out, gtok, gu_out, gg_out, gd_out,
           ag0, ag1, ag2, ag3, pk0, pk1, rw0, rw1, rw2, rw3, wu, wg, wd, part, py0, py1, act0, act1,
           op0, op1, pr0, pr1, pr2, pr3, rs0, rs1, first0, first1, fin0, fin1, fin2, fin3, sel,
           w_sem, sp_send, sp_recv, ag_send, ag_recv, pk_send, rw_recv, y_send, y_recv,
           op_send, pr_recv, rs_send, rs_recv, fin_send, out_recv, g_sem, free):
    ag, pk, rw = (ag0, ag1, ag2, ag3), (pk0, pk1), (rw0, rw1, rw2, rw3)
    py, act = (py0, py1), (act0, act1)
    op, pr = (op0, op1), (pr0, pr1, pr2, pr3)
    rs, first, fin = (rs0, rs1), (first0, first1), (fin0, fin1, fin2, fin3)
    sources, results = (tok, cot), (out, gtok)
    R = S * CAP * ROWS
    SLICE = CHUNKS * ROWS
    seq, y = lax.axis_index("seq"), lax.axis_index("ffn")
    z, s = seq // S, seq % S
    up_z, down_z = lax.rem(z + 1, Z), lax.rem(z + Z - 1, Z)
    toward = (up_z, down_z)
    hops = ((Z // 2, Z - 1 - Z // 2), (Z - 1 - Z // 2, Z // 2))

    def mate(d):
        return lax.rem(s + d, S)

    def in_plane(t):
        return (z * S + t, y)

    def along_z(direction):
        return (toward[direction] * S + s, y)

    def across_y(d):
        return (seq, lax.rem(y + d, Y))

    def each_mate(fn):
        def step(d, carry):
            fn(mate(d))
            return carry
        lax.fori_loop(1, S, step, 0)

    def settle(ref, sem):
        pltpu.make_async_copy(ref, ref, sem).wait()

    def spread(u):
        source, k = sources[u % 2], u // 2

        def piece(t):
            return source.at[pl.ds(pl.multiple_of(t * SLICE + k * ROWS, ROWS), ROWS)]

        def go(t):
            pltpu.make_async_remote_copy(
                src_ref=piece(t), dst_ref=ag[u].at[z * S + s], send_sem=sp_send.at[u], recv_sem=sp_recv.at[u],
                device_id=in_plane(t), device_id_type=MESH).start()
        each_mate(go)
        pltpu.make_async_copy(piece(s), ag[u].at[z * S + s], sp_recv.at[u]).start()

    def ag_copy(u, direction, hop):
        block = lax.rem(z + Z - hop + 1, Z) if direction == 0 else lax.rem(z + hop - 1, Z)
        ref = ag[u].at[pl.ds(block * S, S)]
        return pltpu.make_async_remote_copy(
            src_ref=ref, dst_ref=ref, send_sem=ag_send.at[u, direction, hop - 1],
            recv_sem=ag_recv.at[u, direction, hop - 1], device_id=along_z(direction), device_id_type=MESH)

    def ag_start(u):
        settle(ag[u].at[pl.ds(z * S, S)], sp_recv.at[u])
        for direction in range(2):
            ag_copy(u, direction, 1).start()

    def ag_forward(u, hop):
        for direction in range(2):
            if hop <= hops[u % 2][direction]:
                ag_copy(u, direction, hop - 1).wait_recv()
                ag_copy(u, direction, hop).start()

    def ag_finish(u):
        for direction in range(2):
            ag_copy(u, direction, hops[u % 2][direction]).wait_recv()

    def pack(u):
        a = u % 2
        if u >= 2:
            settle(pk[a].at[pl.ds(0, S - 1)], pk_send.at[u - 2])

        def go(t):
            for j in range(CAP):
                pk[a][t, j] = ag[u][slots[t * CAP + j]]
            pltpu.make_async_remote_copy(
                src_ref=pk[a].at[t], dst_ref=rw[u].at[s], send_sem=pk_send.at[u], recv_sem=rw_recv.at[u],
                device_id=in_plane(t), device_id_type=MESH).start()
        each_mate(go)
        for j in range(CAP):
            rw[u][s, j] = ag[u][slots[s * CAP + j]]

    def rows_ready(u):
        settle(rw[u].at[pl.ds(0, S - 1)], rw_recv.at[u])

    def feature_loop(width, fn):
        def step(b, carry):
            fn(pl.ds(pl.multiple_of(b * width, width), width))
            return carry
        lax.fori_loop(0, W // width, step, 0)

    def wide(ref, columns):
        return ref[:, :, :, columns].reshape(R, columns.size)

    def split(rows):
        return rows.reshape(Y, R // Y, U)

    def up_and_gate(k):
        if k:
            settle(part.at[pl.ds(0, Y - 1)], y_send.at[k - 1, 0])
        part[...] = jnp.zeros_like(part)

        def step(columns):
            x = wide(rw[2 * k], columns)
            part[:, 0] += split(dot(x, wu[columns, :], (1, 0)))
            part[:, 1] += split(dot(x, wg[columns, :], (1, 0)))
        feature_loop(min(512, W), step)

    def hidden_grad(k):
        def step(columns):
            x = wide(rw[2 * k + 1], columns)
            part[:, 2] += split(dot(x, wd[:, columns], (1, 1)))
        feature_loop(min(512, W), step)

    def sum_send(k):
        for d in range(1, Y):
            pltpu.make_async_remote_copy(
                src_ref=part.at[lax.rem(y + d, Y)], dst_ref=py[k].at[d - 1], send_sem=y_send.at[k, 0],
                recv_sem=y_recv.at[k, 0], device_id=across_y(d), device_id_type=MESH).start()

    def activate(k):
        settle(py[k], y_recv.at[k, 0])
        total = [part[y, i] for i in range(3)]
        for d in range(Y - 1):
            total = [total[i] + py[k][d, i] for i in range(3)]
        mask = row_mask[...]
        rectified = jnp.maximum(total[1], 0.0)
        square = rectified * rectified
        grad = total[2] * mask
        act[k][y, 0] = (square * total[0] * mask).astype(BF16)
        act[k][y, 1] = (grad * square).astype(BF16)
        act[k][y, 2] = (grad * total[0] * 2.0 * rectified).astype(BF16)
        for d in range(1, Y):
            pltpu.make_async_remote_copy(
                src_ref=act[k].at[y], dst_ref=act[k].at[y], send_sem=y_send.at[k, 1],
                recv_sem=y_recv.at[k, 1], device_id=across_y(d), device_id_type=MESH).start()

    def act_ready(k):
        settle(act[k].at[pl.ds(0, Y - 1)], y_recv.at[k, 1])

    def activation(k, i):
        return act[k][:, i].reshape(R, U)

    def give_back(u):
        a = u % 2

        def go(t):
            pltpu.make_async_remote_copy(
                src_ref=op[a].at[t], dst_ref=pr[u].at[s], send_sem=op_send.at[u], recv_sem=pr_recv.at[u],
                device_id=in_plane(t), device_id_type=MESH).start()
        each_mate(go)
        pltpu.make_async_copy(op[a].at[s], pr[u].at[s], pr_recv.at[u]).start()

    def down(k):
        u = 2 * k
        if k:
            settle(op[0].at[pl.ds(0, S - 1)], op_send.at[u - 2])

        def step(columns):
            product = dot(activation(k, 0), wd[:, columns], (1, 0))
            op[0][:, :, :, columns] = product.astype(BF16).reshape(S, CAP, ROWS, columns.size)
        feature_loop(min(512, W), step)
        give_back(u)

    def back(k):
        u = 2 * k + 1
        if k:
            settle(op[1].at[pl.ds(0, S - 1)], op_send.at[u - 2])

        def step(columns):
            product = dot(activation(k, 1), wu[columns, :], (1, 1))
            product = product + dot(activation(k, 2), wg[columns, :], (1, 1))
            op[1][:, :, :, columns] = product.astype(BF16).reshape(S, CAP, ROWS, columns.size)
        feature_loop(min(512, W), step)
        give_back(u)

    def collected(u):
        settle(pr[u], pr_recv.at[u])

    def plane_sum(u, target, columns):
        pick = sel[pl.ds(pl.multiple_of(target * (S * ROWS), S * ROWS), S * ROWS), :]
        return dot(pick, wide(pr[u], columns), (1, 0)).reshape(S, ROWS, columns.size)

    def slot_of(a, direction, hop):
        return hop - 1 + (hops[a][0] if direction else 0)

    def rs_copy(u, direction, hop):
        a = u % 2
        source = first[a].at[direction] if hop == 1 else rs[a].at[slot_of(a, direction, hop - 1)]
        return pltpu.make_async_remote_copy(
            src_ref=source, dst_ref=rs[a].at[slot_of(a, direction, hop)],
            send_sem=rs_send.at[u, direction, hop - 1], recv_sem=rs_recv.at[u, direction, hop - 1],
            device_id=along_z(direction), device_id_type=MESH)

    def release(u, direction):
        if u < 2:
            pl.semaphore_signal(free.at[u, direction], inc=1, device_id=along_z(1 - direction), device_id_type=MESH)

    def rs_step(u, direction, hop):
        a = u % 2
        last = hops[a][direction]
        if hop > last:
            return
        far = last - hop + 1
        target = lax.rem(z + far, Z) if direction == 0 else lax.rem(z + Z - far, Z)
        if hop == 1:
            if u >= 2:
                rs_copy(u - 2, direction, 1).wait_send()

            def step(columns):
                first[a][direction, :, :, columns] = plane_sum(u, target, columns).astype(BF16)
        else:
            if hop > 2:
                rs_copy(u, direction, hop - 1).wait_send()
                release(u, direction)
            rs_copy(u, direction, hop - 1).wait_recv()
            at = slot_of(a, direction, hop - 1)

            def step(columns):
                total = rs[a][at, :, :, columns].astype(F32) + plane_sum(u, target, columns)
                rs[a][at, :, :, columns] = total.astype(BF16)
        feature_loop(min(512, W), step)
        if u >= 2:
            pl.semaphore_wait(free.at[u - 2, direction], 1)
        rs_copy(u, direction, hop).start()

    def rs_both(u, hop):
        for direction in range(2):
            rs_step(u, direction, hop)

    def finish(u):
        a, k = u % 2, u // 2
        ends = []
        for direction in range(2):
            last = hops[a][direction]
            if last > 1:
                rs_copy(u, direction, last).wait_send()
                release(u, direction)
            rs_copy(u, direction, last).wait_recv()
            ends.append(slot_of(a, direction, last))

        def step(columns):
            total = plane_sum(u, z, columns)
            for at in ends:
                total = total + rs[a][at, :, :, columns].astype(F32)
            fin[u][:, :, columns] = total.astype(BF16)
        feature_loop(min(512, W), step)
        for direction in range(2):
            release(u, direction)
        place = results[a].at[pl.ds(pl.multiple_of(s * SLICE + k * ROWS, ROWS), ROWS)]

        def go(t):
            pltpu.make_async_remote_copy(
                src_ref=fin[u].at[t], dst_ref=place, send_sem=fin_send.at[u], recv_sem=out_recv.at[u],
                device_id=in_plane(t), device_id_type=MESH).start()
        each_mate(go)
        pltpu.make_async_copy(fin[u].at[s], place, out_recv.at[u]).start()

    def token_weight_grad(i, buffer, target):
        width = min(256, W)

        def step(b, carry):
            columns = pl.ds(pl.multiple_of(b * width, width), width)
            total = dot(wide(rw[0], columns), activation(0, i), (0, 0))
            total = total + dot(wide(rw[2], columns), activation(1, i), (0, 0))
            buffer[columns, :] = (total * grad_scale).astype(BF16)
            return carry
        lax.fori_loop(0, W // width, step, 0)
        pltpu.make_async_copy(buffer, target, g_sem.at[i]).start()

    def down_weight_grad(buffer, target):
        width = min(256, W)

        def step(columns):
            total = dot(activation(0, 0), wide(rw[1], columns), (0, 0))
            total = total + dot(activation(1, 0), wide(rw[3], columns), (0, 0))
            buffer[:, columns] = (total * grad_scale).astype(BF16)
        feature_loop(width, step)
        pltpu.make_async_copy(buffer, target, g_sem.at[0]).start()

    grad_scale = 1.0 / (S * SLICE)
    weights = [pltpu.make_async_copy(wu_in, wu, w_sem.at[0]), pltpu.make_async_copy(wg_in, wg, w_sem.at[1]),
               pltpu.make_async_copy(wd_in, wd, w_sem.at[2])]
    for copy in weights:
        copy.start()

    barrier = pltpu.get_barrier_semaphore()

    def greet(device):
        pl.semaphore_signal(barrier, inc=1, device_id=device, device_id_type=MESH)
    each_mate(lambda t: greet(in_plane(t)))
    for direction in range(2):
        greet(along_z(direction))
    for d in range(1, Y):
        greet(across_y(d))
    pl.semaphore_wait(barrier, S - 1 + 2 + Y - 1)

    for u in range(4):
        spread(u)
    ag_start(0)
    ag_start(1)

    def select_rows(g, carry):
        row = lax.broadcasted_iota(jnp.int32, (ROWS, R), 0)
        column = lax.broadcasted_iota(jnp.int32, (ROWS, R), 1)
        hit = (column_group[...] == g) & (lax.rem(column, ROWS) == row)
        sel[pl.ds(pl.multiple_of(g * ROWS, ROWS), ROWS), :] = jnp.where(hit, 1.0, 0.0).astype(BF16)
        return carry
    lax.fori_loop(0, Z * S, select_rows, 0)
    for copy in weights:
        copy.wait()

    far = max(hops[0])
    for hop in range(2, far + 1):
        ag_forward(0, hop)
        ag_forward(1, hop)
    ag_start(2)
    ag_start(3)

    def chunk_steps(k):
        t, c = 2 * k, 2 * k + 1
        return [
            lambda: (ag_finish(t), pack(t), ag_finish(c), pack(c)),
            lambda: (rows_ready(t), up_and_gate(k)),
            lambda: (rows_ready(c), hidden_grad(k), sum_send(k)),
            lambda: activate(k),
            lambda: (act_ready(k), down(k)),
            lambda: back(k),
        ]

    def weave(main, beside):
        n = max(len(main), len(beside))
        for i in range(n):
            if i < len(main):
                main[i]()
            if i < len(beside):
                beside[i]()

    weave(chunk_steps(0), [functools.partial(ag_forward, u, hop) for hop in range(2, far + 1) for u in (2, 3)])
    for u in (0, 1):
        collected(u)
        rs_both(u, 1)
    weave(chunk_steps(1), [functools.partial(rs_both, u, hop) for hop in range(2, far + 1) for u in (0, 1)])
    finish(0)
    finish(1)
    for u in (2, 3):
        collected(u)
        rs_both(u, 1)
    weave([functools.partial(token_weight_grad, 1, wu, gu_out), functools.partial(token_weight_grad, 2, wg, gg_out),
           functools.partial(down_weight_grad, wd, gd_out)],
          [functools.partial(rs_both, u, hop) for hop in range(2, far + 1) for u in (2, 3)])
    finish(2)
    finish(3)

    for u in range(4):
        a, k = u % 2, u // 2
        settle(sources[a].at[pl.ds(0, (S - 1) * ROWS)], sp_send.at[u])
        for direction in range(2):
            for hop in range(1, hops[a][direction] + 1):
                ag_copy(u, direction, hop).wait_send()
        settle(fin[u].at[pl.ds(0, S - 1)], fin_send.at[u])
        settle(results[a].at[pl.ds(0, S * ROWS)], out_recv.at[u])
    for u in (2, 3):
        a = u % 2
        settle(pk[a].at[pl.ds(0, S - 1)], pk_send.at[u])
        settle(op[a].at[pl.ds(0, S - 1)], op_send.at[u])
        for direction in range(2):
            rs_copy(u, direction, 1).wait_send()
    settle(part.at[pl.ds(0, Y - 1)], y_send.at[1, 0])
    for k in range(CHUNKS):
        settle(act[k].at[pl.ds(0, Y - 1)], y_send.at[k, 1])
    for i, (buffer, target) in enumerate(((wd, gd_out), (wu, gu_out), (wg, gg_out))):
        pltpu.make_async_copy(buffer, target, g_sem.at[i]).wait()


def body(tokens, cotangent, block_masks, w_up, w_gate, w_down):
    owners, Y = lax.axis_size("seq"), lax.axis_size("ffn")
    S, Z = PLANE, owners // PLANE
    _, group_len, W = tokens.shape
    groups = block_masks.shape[0]
    U = w_up.shape[1]
    owner_blocks = U // BLK
    R = S * CAP * ROWS
    my_owner = lax.axis_index("seq")
    first_owner = (my_owner // S) * S
    mine = lax.dynamic_slice_in_dim(block_masks, first_owner * owner_blocks, S * owner_blocks, 1)
    active = jnp.max(mine.reshape(groups, S, owner_blocks), axis=2).T
    ordinal = jnp.cumsum(active, axis=1) - 1
    slot_ids = jnp.arange(CAP, dtype=jnp.int32)
    picked = (ordinal[:, None, :] == slot_ids[None, :, None]) & (active[:, None, :] > 0)
    group_ids = jnp.arange(groups, dtype=jnp.int32)
    slot_group = jnp.sum(jnp.where(picked, group_ids, 0), axis=2).reshape(-1)
    held_group = jnp.where(jnp.any(picked, axis=2).reshape(-1), slot_group, -1)
    column_group = jnp.repeat(held_group, ROWS).reshape(1, R)
    my_picked = lax.dynamic_index_in_dim(picked, my_owner % S, 0, keepdims=False)
    my_columns = lax.dynamic_slice_in_dim(block_masks, my_owner * owner_blocks, owner_blocks, 1)
    block_live = jnp.sum(jnp.where(my_picked[:, :, None], my_columns[None], 0), axis=1).astype(F32)
    unit_live = jnp.repeat(block_live, BLK, axis=1)
    quarter = R // Y
    row_mask = jnp.broadcast_to(
        unit_live[None, :, None, :], (quarter // (CAP * ROWS), CAP, ROWS, U)).reshape(quarter, U)

    hbm, vmem = pl.BlockSpec(memory_space=pl.ANY), pl.BlockSpec(memory_space=pltpu.VMEM)
    half = Z // 2
    rows = pltpu.VMEM((S, CAP, ROWS, W), BF16)
    gathered = pltpu.VMEM((Z * S, ROWS, W), BF16)
    dma = pltpu.SemaphoreType.DMA
    scratch = (
        [gathered] * 4 + [rows] * 2 + [rows] * 4
        + [pltpu.VMEM((W, U), BF16)] * 2 + [pltpu.VMEM((U, W), BF16)]
        + [pltpu.VMEM((Y, 3, quarter, U), F32)]
        + [pltpu.VMEM((Y - 1, 3, quarter, U), F32)] * 2
        + [pltpu.VMEM((Y, 3, quarter, U), BF16)] * 2
        + [rows] * 2 + [rows] * 4
        + [pltpu.VMEM((Z - 1, S, ROWS, W), BF16)] * 2
        + [pltpu.VMEM((2, S, ROWS, W), BF16)] * 2
        + [pltpu.VMEM((S, ROWS, W), BF16)] * 4
        + [pltpu.VMEM((Z * S * ROWS, R), BF16)]
        + [
            dma((3,)), dma((4,)), dma((4,)), dma((4, 2, half)), dma((4, 2, half)), dma((4,)), dma((4,)),
            dma((2, 2)), dma((2, 2)), dma((4,)), dma((4,)), dma((4, 2, half)), dma((4, 2, half)), dma((4,)),
            dma((4,)), dma((3,)), pltpu.SemaphoreType.REGULAR((2, 2)),
        ]
    )
    shapes = (
        jax.ShapeDtypeStruct((group_len, W), BF16), jax.ShapeDtypeStruct((group_len, W), BF16),
        jax.ShapeDtypeStruct((W, U), BF16), jax.ShapeDtypeStruct((W, U), BF16), jax.ShapeDtypeStruct((U, W), BF16),
    )
    outputs, grad_tokens, grad_up, grad_gate, grad_down = pl.pallas_call(
        functools.partial(kernel, Z, S, Y, W, U),
        out_shape=shapes,
        in_specs=[pl.BlockSpec(memory_space=pltpu.SMEM), vmem, vmem] + [hbm] * 5,
        out_specs=[hbm] * 5,
        scratch_shapes=scratch,
        compiler_params=pltpu.CompilerParams(
            collective_id=0, has_side_effects=True, vmem_limit_bytes=63 * 1024 * 1024),
        cost_estimate=pl.CostEstimate(flops=18 * CHUNKS * R * W * U, bytes_accessed=10 * 2**20, transcendentals=0),
    )(slot_group, column_group, row_mask, tokens.reshape(group_len, W), cotangent.reshape(group_len, W),
      w_up, w_gate, w_down)
    return outputs[None], grad_tokens[None], grad_up, grad_gate, grad_down


def solution(mesh):
    in_specs = (
        P("seq", None, "ffn"),
        P("seq", None, "ffn"),
        P(),
        P("ffn", "seq"),
        P("ffn", "seq"),
        P("seq", "ffn"),
    )
    out_specs = (
        P("seq", None, "ffn"),
        P("seq", None, "ffn"),
        P("ffn", "seq"),
        P("ffn", "seq"),
        P("seq", "ffn"),
    )
    return jax.shard_map(body, mesh=mesh, in_specs=in_specs, out_specs=out_specs, check_vma=False)
```

```python
import functools

import jax
import jax.numpy as jnp
from jax import lax
from jax.experimental import pallas as pl
from jax.experimental.pallas import tpu as pltpu
from jax.sharding import PartitionSpec as P

BLK = 128
CAP = 3
PLANE = 8
ROWS = 16
CHUNKS = 2
MESH = pl.DeviceIdType.MESH
F32, BF16 = jnp.float32, jnp.bfloat16


def dot(left, right, dims):
    return lax.dot_general(left, right, (((dims[0],), (dims[1],)), ((), ())), preferred_element_type=F32)


def offsets(caps, hops, S):
    at, table = S, []
    for direction in range(2):
        row = []
        for count in caps[hops[direction]]:
            row.append(at)
            at += count
        table.append(row)
    return table, at


def hop_counts(Z):
    far, near = Z // 2, Z - 1 - Z // 2
    return ((far, near), (near, far))


def kernel(Z, S, Y, W, U, caps, slots, sums, orders, column_group, row_mask, tok, cot, wu_in, wg_in, wd_in,
           out, gtok, gu_out, gg_out, gd_out,
           ag0, ag1, ag2, ag3, so0, so1, so2, so3, pk0, pk1, rw0, rw1, rw2, rw3, wu, wg, wd, part, py0, py1, act0, act1,
           op0, op1, pr0, pr1, pr2, pr3, rs0, rs1, f00, f01, f10, f11, fin0, fin1, fin2, fin3, sel,
           sort0, sort1, sort2, sort3,
           w_sem, sp_send, sp_recv, ag_send, ag_recv, pk_send, rw_recv, y_send, y_recv,
           op_send, pr_recv, rs_send, rs_recv, fin_send, out_recv, g_sem, free):
    ag, pk, rw = (ag0, ag1, ag2, ag3), (pk0, pk1), (rw0, rw1, rw2, rw3)
    py, act = (py0, py1), (act0, act1)
    op, pr = (op0, op1), (pr0, pr1, pr2, pr3)
    rs, first, fin = (rs0, rs1), ((f00, f01), (f10, f11)), (fin0, fin1, fin2, fin3)
    sorted_rows, sort = ((so0, so1), (so2, so3)), ((sort0, sort1), (sort2, sort3))
    sources, results = (tok, cot), (out, gtok)
    R = S * CAP * ROWS
    SLICE = CHUNKS * ROWS
    seq, y = lax.axis_index("seq"), lax.axis_index("ffn")
    z, s = seq // S, seq % S
    up_z, down_z = lax.rem(z + 1, Z), lax.rem(z + Z - 1, Z)
    toward = (up_z, down_z)
    hops = hop_counts(Z)
    blocks = [offsets(caps, hops[a], S)[0] for a in range(2)]

    def mate(d):
        return lax.rem(s + d, S)

    def in_plane(t):
        return (z * S + t, y)

    def along_z(direction):
        return (toward[direction] * S + s, y)

    def across_y(d):
        return (seq, lax.rem(y + d, Y))

    def each_mate(fn):
        def step(d, carry):
            fn(mate(d))
            return carry
        lax.fori_loop(1, S, step, 0)

    def settle(ref, sem):
        pltpu.make_async_copy(ref, ref, sem).wait()

    def spread(u):
        source, k = sources[u % 2], u // 2

        def piece(t):
            return source.at[pl.ds(pl.multiple_of(t * SLICE + k * ROWS, ROWS), ROWS)]

        def go(t):
            pltpu.make_async_remote_copy(
                src_ref=piece(t), dst_ref=ag[u].at[s], send_sem=sp_send.at[u], recv_sem=sp_recv.at[u],
                device_id=in_plane(t), device_id_type=MESH).start()
        each_mate(go)
        pltpu.make_async_copy(piece(s), ag[u].at[s], sp_recv.at[u]).start()

    def arrivals(a, direction, hop, count):
        return pl.ds(blocks[a][direction][hop - 1], count)

    def ag_copy(u, direction, hop):
        a = u % 2
        count = caps[hops[a][direction]][hop - 1]
        source = sorted_rows[a][direction] if hop == 1 else ag[u].at[arrivals(a, direction, hop - 1, count)]
        return pltpu.make_async_remote_copy(
            src_ref=source, dst_ref=ag[u].at[arrivals(a, direction, hop, count)],
            send_sem=ag_send.at[u, direction, hop - 1], recv_sem=ag_recv.at[u, direction, hop - 1],
            device_id=along_z(direction), device_id_type=MESH)

    def ag_start(u):
        a = u % 2
        settle(ag[u].at[pl.ds(0, S)], sp_recv.at[u])
        for direction in range(2):
            target = sorted_rows[a][direction]
            if u >= 2:
                ag_copy(u - 2, direction, 1).wait_send()

            def step(columns):
                own = ag[u][0:S, :, columns].reshape(S * ROWS, columns.size)
                moved = dot(sort[a][direction][...], own, (1, 0)).astype(BF16)
                target[:, :, columns] = moved.reshape(target.shape[0], ROWS, columns.size)
            feature_loop(min(512, W), step)
            ag_copy(u, direction, 1).start()

    def ag_forward(u, hop):
        for direction in range(2):
            if hop <= hops[u % 2][direction]:
                ag_copy(u, direction, hop - 1).wait_recv()
                ag_copy(u, direction, hop).start()

    def ag_finish(u):
        for direction in range(2):
            ag_copy(u, direction, hops[u % 2][direction]).wait_recv()

    def pack(u):
        a = u % 2
        if u >= 2:
            settle(pk[a].at[pl.ds(0, S - 1)], pk_send.at[u - 2])

        def go(t):
            for j in range(CAP):
                pk[a][t, j] = ag[u][slots[a, t * CAP + j]]
            pltpu.make_async_remote_copy(
                src_ref=pk[a].at[t], dst_ref=rw[u].at[s], send_sem=pk_send.at[u], recv_sem=rw_recv.at[u],
                device_id=in_plane(t), device_id_type=MESH).start()
        each_mate(go)
        for j in range(CAP):
            rw[u][s, j] = ag[u][slots[a, s * CAP + j]]

    def rows_ready(u):
        settle(rw[u].at[pl.ds(0, S - 1)], rw_recv.at[u])

    def feature_loop(width, fn):
        def step(b, carry):
            fn(pl.ds(pl.multiple_of(b * width, width), width))
            return carry
        lax.fori_loop(0, W // width, step, 0)

    def wide(ref, columns):
        return ref[:, :, :, columns].reshape(R, columns.size)

    def split(rows):
        return rows.reshape(Y, R // Y, U)

    def up_and_gate(k):
        if k:
            settle(part.at[pl.ds(0, Y - 1)], y_send.at[k - 1, 0])
        part[...] = jnp.zeros_like(part)

        def step(columns):
            x = wide(rw[2 * k], columns)
            part[:, 0] += split(dot(x, wu[columns, :], (1, 0)))
            part[:, 1] += split(dot(x, wg[columns, :], (1, 0)))
        feature_loop(min(512, W), step)

    def hidden_grad(k):
        def step(columns):
            x = wide(rw[2 * k + 1], columns)
            part[:, 2] += split(dot(x, wd[:, columns], (1, 1)))
        feature_loop(min(512, W), step)

    def sum_send(k):
        for d in range(1, Y):
            pltpu.make_async_remote_copy(
                src_ref=part.at[lax.rem(y + d, Y)], dst_ref=py[k].at[d - 1], send_sem=y_send.at[k, 0],
                recv_sem=y_recv.at[k, 0], device_id=across_y(d), device_id_type=MESH).start()

    def activate(k):
        settle(py[k], y_recv.at[k, 0])
        total = [part[y, i] for i in range(3)]
        for d in range(Y - 1):
            total = [total[i] + py[k][d, i] for i in range(3)]
        mask = row_mask[...]
        rectified = jnp.maximum(total[1], 0.0)
        square = rectified * rectified
        grad = total[2] * mask
        act[k][y, 0] = (square * total[0] * mask).astype(BF16)
        act[k][y, 1] = (grad * square).astype(BF16)
        act[k][y, 2] = (grad * total[0] * 2.0 * rectified).astype(BF16)
        for d in range(1, Y):
            pltpu.make_async_remote_copy(
                src_ref=act[k].at[y], dst_ref=act[k].at[y], send_sem=y_send.at[k, 1],
                recv_sem=y_recv.at[k, 1], device_id=across_y(d), device_id_type=MESH).start()

    def act_ready(k):
        settle(act[k].at[pl.ds(0, Y - 1)], y_recv.at[k, 1])

    def activation(k, i):
        return act[k][:, i].reshape(R, U)

    def give_back(u):
        a = u % 2

        def go(t):
            pltpu.make_async_remote_copy(
                src_ref=op[a].at[t], dst_ref=pr[u].at[s], send_sem=op_send.at[u], recv_sem=pr_recv.at[u],
                device_id=in_plane(t), device_id_type=MESH).start()
        each_mate(go)
        pltpu.make_async_copy(op[a].at[s], pr[u].at[s], pr_recv.at[u]).start()

    def down(k):
        u = 2 * k
        if k:
            settle(op[0].at[pl.ds(0, S - 1)], op_send.at[u - 2])

        def step(columns):
            product = dot(activation(k, 0), wd[:, columns], (1, 0))
            op[0][:, :, :, columns] = product.astype(BF16).reshape(S, CAP, ROWS, columns.size)
        feature_loop(min(512, W), step)
        give_back(u)

    def back(k):
        u = 2 * k + 1
        if k:
            settle(op[1].at[pl.ds(0, S - 1)], op_send.at[u - 2])

        def step(columns):
            product = dot(activation(k, 1), wu[columns, :], (1, 1))
            product = product + dot(activation(k, 2), wg[columns, :], (1, 1))
            op[1][:, :, :, columns] = product.astype(BF16).reshape(S, CAP, ROWS, columns.size)
        feature_loop(min(512, W), step)
        give_back(u)

    def collected(u):
        settle(pr[u], pr_recv.at[u])

    sum_rows = [S * ROWS]
    sum_at = []
    for a in range(2):
        sum_at.append([])
        for direction in range(2):
            row = []
            for count in caps[hops[a][direction]]:
                row.append(sum_rows[0])
                sum_rows[0] += count * ROWS
            sum_at[a].append(row)

    def plane_sum(u, direction, far, columns):
        a = u % 2
        at, count = (0, S) if far == 0 else (sum_at[a][direction][far - 1], caps[hops[a][direction]][far - 1])
        pick = sel[at:at + count * ROWS, :]
        return dot(pick, wide(pr[u], columns), (1, 0)).reshape(count, ROWS, columns.size)

    room = []
    for a in range(2):
        at, table = 0, []
        for direction in range(2):
            row, counts = [], caps[hops[a][direction]]
            for hop in range(1, len(counts) + 1):
                row.append(at)
                at += counts[max(len(counts) - hop, 1) - 1]
            table.append(row)
        room.append(table)

    def received(a, direction, hop, count):
        return rs[a].at[pl.ds(room[a][direction][hop - 1], count)]

    def rs_copy(u, direction, hop):
        a = u % 2
        counts = caps[hops[a][direction]]
        count = counts[len(counts) - hop]
        source = first[a][direction] if hop == 1 else received(a, direction, hop - 1, count)
        return pltpu.make_async_remote_copy(
            src_ref=source, dst_ref=received(a, direction, hop, count),
            send_sem=rs_send.at[u, direction, hop - 1], recv_sem=rs_recv.at[u, direction, hop - 1],
            device_id=along_z(direction), device_id_type=MESH)

    def release(u, direction):
        if u < 2:
            pl.semaphore_signal(free.at[u, direction], inc=1, device_id=along_z(1 - direction), device_id_type=MESH)

    def rs_step(u, direction, hop):
        a = u % 2
        last = hops[a][direction]
        if hop > last:
            return
        far = last - hop + 1
        if hop == 1:
            if u >= 2:
                rs_copy(u - 2, direction, 1).wait_send()

            def step(columns):
                first[a][direction][:, :, columns] = plane_sum(u, direction, far, columns).astype(BF16)
        else:
            if hop > 2:
                rs_copy(u, direction, hop - 1).wait_send()
                release(u, direction)
            rs_copy(u, direction, hop - 1).wait_recv()
            old = caps[last][far]
            arrived = received(a, direction, hop - 1, old)
            fresh = rs[a].at[pl.ds(room[a][direction][hop - 2] + old, caps[last][far - 1] - old)]

            def step(columns):
                total = plane_sum(u, direction, far, columns)
                arrived[:, :, columns] = (arrived[:, :, columns].astype(F32) + total[:old]).astype(BF16)
                if caps[last][far - 1] > old:
                    fresh[:, :, columns] = total[old:].astype(BF16)
        feature_loop(min(512, W), step)
        if u >= 2:
            pl.semaphore_wait(free.at[u - 2, direction], 1)
        rs_copy(u, direction, hop).start()

    def rs_both(u, hop):
        for direction in range(2):
            rs_step(u, direction, hop)

    def finish(u):
        a, k = u % 2, u // 2
        ends = []
        for direction in range(2):
            last = hops[a][direction]
            if last > 1:
                rs_copy(u, direction, last).wait_send()
                release(u, direction)
            rs_copy(u, direction, last).wait_recv()
            ends.append(received(a, direction, last, caps[last][0]))

        def step(columns):
            total = plane_sum(u, 0, 0, columns)
            for direction in range(2):
                arrived = ends[direction][:, :, columns].reshape(-1, columns.size)
                total = total + dot(sort[1 - a][1 - direction][...], arrived, (0, 0)).reshape(S, ROWS, columns.size)
            fin[u][:, :, columns] = total.astype(BF16)
        feature_loop(min(512, W), step)
        for direction in range(2):
            release(u, direction)
        place = results[a].at[pl.ds(pl.multiple_of(s * SLICE + k * ROWS, ROWS), ROWS)]

        def go(t):
            pltpu.make_async_remote_copy(
                src_ref=fin[u].at[t], dst_ref=place, send_sem=fin_send.at[u], recv_sem=out_recv.at[u],
                device_id=in_plane(t), device_id_type=MESH).start()
        each_mate(go)
        pltpu.make_async_copy(fin[u].at[s], place, out_recv.at[u]).start()

    def token_weight_grad(i, buffer, target):
        width = min(256, W)

        def step(b, carry):
            columns = pl.ds(pl.multiple_of(b * width, width), width)
            total = dot(wide(rw[0], columns), activation(0, i), (0, 0))
            total = total + dot(wide(rw[2], columns), activation(1, i), (0, 0))
            buffer[columns, :] = (total * grad_scale).astype(BF16)
            return carry
        lax.fori_loop(0, W // width, step, 0)
        pltpu.make_async_copy(buffer, target, g_sem.at[i]).start()

    def down_weight_grad(buffer, target):
        width = min(256, W)

        def step(columns):
            total = dot(activation(0, 0), wide(rw[1], columns), (0, 0))
            total = total + dot(activation(1, 0), wide(rw[3], columns), (0, 0))
            buffer[:, columns] = (total * grad_scale).astype(BF16)
        feature_loop(width, step)
        pltpu.make_async_copy(buffer, target, g_sem.at[0]).start()

    grad_scale = 1.0 / (S * SLICE)
    weights = [pltpu.make_async_copy(wu_in, wu, w_sem.at[0]), pltpu.make_async_copy(wg_in, wg, w_sem.at[1]),
               pltpu.make_async_copy(wd_in, wd, w_sem.at[2])]
    for copy in weights:
        copy.start()

    barrier = pltpu.get_barrier_semaphore()

    def greet(device):
        pl.semaphore_signal(barrier, inc=1, device_id=device, device_id_type=MESH)
    each_mate(lambda t: greet(in_plane(t)))
    for direction in range(2):
        greet(along_z(direction))
    for d in range(1, Y):
        greet(across_y(d))
    pl.semaphore_wait(barrier, S - 1 + 2 + Y - 1)

    for u in range(4):
        spread(u)
    for a in range(2):
        for direction in range(2):
            for r in range(caps[hops[a][direction]][0]):
                row = lax.broadcasted_iota(jnp.int32, (ROWS, S * ROWS), 0)
                column = lax.broadcasted_iota(jnp.int32, (ROWS, S * ROWS), 1)
                hit = column == orders[2 * a + direction, r] * ROWS + row
                sort[a][direction][r * ROWS:(r + 1) * ROWS, :] = jnp.where(hit, 1.0, 0.0).astype(BF16)
    ag_start(0)
    ag_start(1)

    def select_rows(g, carry):
        row = lax.broadcasted_iota(jnp.int32, (ROWS, R), 0)
        column = lax.broadcasted_iota(jnp.int32, (ROWS, R), 1)
        hit = (column_group[...] == sums[g]) & (lax.rem(column, ROWS) == row)
        sel[pl.ds(pl.multiple_of(g * ROWS, ROWS), ROWS), :] = jnp.where(hit, 1.0, 0.0).astype(BF16)
        return carry
    lax.fori_loop(0, sum_rows[0] // ROWS, select_rows, 0)
    for copy in weights:
        copy.wait()

    far = max(hops[0])
    for hop in range(2, far + 1):
        ag_forward(0, hop)
        ag_forward(1, hop)
    ag_start(2)
    ag_start(3)

    def chunk_steps(k):
        t, c = 2 * k, 2 * k + 1
        return [
            lambda: (ag_finish(t), pack(t), ag_finish(c), pack(c)),
            lambda: (rows_ready(t), up_and_gate(k)),
            lambda: (rows_ready(c), hidden_grad(k), sum_send(k)),
            lambda: activate(k),
            lambda: (act_ready(k), down(k)),
            lambda: back(k),
        ]

    def weave(main, beside):
        n = max(len(main), len(beside))
        for i in range(n):
            if i < len(main):
                main[i]()
            if i < len(beside):
                beside[i]()

    weave(chunk_steps(0), [functools.partial(ag_forward, u, hop) for hop in range(2, far + 1) for u in (2, 3)])
    for u in (0, 1):
        collected(u)
        rs_both(u, 1)
    weave(chunk_steps(1), [functools.partial(rs_both, u, hop) for hop in range(2, far + 1) for u in (0, 1)])
    finish(0)
    finish(1)
    for u in (2, 3):
        collected(u)
        rs_both(u, 1)
    weave([functools.partial(token_weight_grad, 1, wu, gu_out), functools.partial(token_weight_grad, 2, wg, gg_out),
           functools.partial(down_weight_grad, wd, gd_out)],
          [functools.partial(rs_both, u, hop) for hop in range(2, far + 1) for u in (2, 3)])
    finish(2)
    finish(3)

    for u in range(4):
        a, k = u % 2, u // 2
        settle(sources[a].at[pl.ds(0, (S - 1) * ROWS)], sp_send.at[u])
        for direction in range(2):
            for hop in range(1 if k else 2, hops[a][direction] + 1):
                ag_copy(u, direction, hop).wait_send()
        settle(fin[u].at[pl.ds(0, S - 1)], fin_send.at[u])
        settle(results[a].at[pl.ds(0, S * ROWS)], out_recv.at[u])
    for u in (2, 3):
        a = u % 2
        settle(pk[a].at[pl.ds(0, S - 1)], pk_send.at[u])
        settle(op[a].at[pl.ds(0, S - 1)], op_send.at[u])
        for direction in range(2):
            rs_copy(u, direction, 1).wait_send()
    settle(part.at[pl.ds(0, Y - 1)], y_send.at[1, 0])
    for k in range(CHUNKS):
        settle(act[k].at[pl.ds(0, Y - 1)], y_send.at[k, 1])
    for i, (buffer, target) in enumerate(((wd, gd_out), (wu, gu_out), (wg, gg_out))):
        pltpu.make_async_copy(buffer, target, g_sem.at[i]).wait()


def levels(Z, S):
    far = Z // 2
    full = {far: (S,) * far, Z - 1 - far: (S,) * (Z - 1 - far)}
    if (Z, S) != (8, 8):
        return [full]
    return [{4: (7, 6, 5, 3), 3: (6, 5, 4)}, {4: (8, 7, 6, 4), 3: (7, 6, 4)}, full]


def ffn(level, caps, Z, S, Y, U, held_group, slot_place, sum_orders, sort_orders, row_mask, tokens, cotangent,
        w_up, w_gate, w_down):
    group_len, W = tokens.shape
    R = S * CAP * ROWS
    quarter = R // Y
    hops = hop_counts(Z)
    start = [offsets(caps, hops[a], S) for a in range(2)]
    slots = []
    for a in range(2):
        away, rank = slot_place[a]
        first = jnp.asarray([0] + start[a][0][0] + start[a][0][1][::-1], jnp.int32)
        slots.append(jnp.sum(jnp.where(away[:, None] == jnp.arange(Z)[None, :], first[None, :], 0), axis=1) + rank)
    slots = jnp.stack(slots).astype(jnp.int32)
    sums = [sum_orders[0]]
    for a in range(2):
        for direction in range(2):
            for far, count in enumerate(caps[hops[a][direction]]):
                sums.append(sum_orders[1][a][direction][far][:count])
    sums = jnp.concatenate(sums).astype(jnp.int32)
    column_group = jnp.repeat(held_group, ROWS).reshape(1, R)

    hbm, vmem = pl.BlockSpec(memory_space=pl.ANY), pl.BlockSpec(memory_space=pltpu.VMEM)
    smem = pl.BlockSpec(memory_space=pltpu.SMEM)
    half = Z // 2
    rows = pltpu.VMEM((S, CAP, ROWS, W), BF16)
    dma = pltpu.SemaphoreType.DMA

    def groups_of(count):
        return pltpu.VMEM((count, ROWS, W), BF16)

    def counts(a, direction):
        return caps[hops[a][direction]]
    ways = [(a, direction) for a in range(2) for direction in range(2)]
    room = [sum(sum(counts(a, d)[max(len(counts(a, d)) - hop, 1) - 1] for hop in range(1, len(counts(a, d)) + 1))
                for d in range(2)) for a in range(2)]
    scratch = (
        [groups_of(start[u % 2][1]) for u in range(4)]
        + [groups_of(counts(a, d)[0]) for a, d in ways]
        + [rows] * 2 + [rows] * 4
        + [pltpu.VMEM((W, U), BF16)] * 2 + [pltpu.VMEM((U, W), BF16)]
        + [pltpu.VMEM((Y, 3, quarter, U), F32)]
        + [pltpu.VMEM((Y - 1, 3, quarter, U), F32)] * 2
        + [pltpu.VMEM((Y, 3, quarter, U), BF16)] * 2
        + [rows] * 2 + [rows] * 4
        + [groups_of(room[a]) for a in range(2)]
        + [groups_of(counts(a, d)[-1]) for a, d in ways]
        + [groups_of(S)] * 4
        + [pltpu.VMEM((sums.shape[0] * ROWS, R), BF16)]
        + [pltpu.VMEM((counts(a, d)[0] * ROWS, S * ROWS), BF16) for a, d in ways]
        + [
            dma((3,)), dma((4,)), dma((4,)), dma((4, 2, half)), dma((4, 2, half)), dma((4,)), dma((4,)),
            dma((2, 2)), dma((2, 2)), dma((4,)), dma((4,)), dma((4, 2, half)), dma((4, 2, half)), dma((4,)),
            dma((4,)), dma((3,)), pltpu.SemaphoreType.REGULAR((2, 2)),
        ]
    )
    shapes = (
        jax.ShapeDtypeStruct((group_len, W), BF16), jax.ShapeDtypeStruct((group_len, W), BF16),
        jax.ShapeDtypeStruct((W, U), BF16), jax.ShapeDtypeStruct((W, U), BF16), jax.ShapeDtypeStruct((U, W), BF16),
    )
    return pl.pallas_call(
        functools.partial(kernel, Z, S, Y, W, U, caps),
        out_shape=shapes,
        in_specs=[smem] * 3 + [vmem] * 2 + [hbm] * 5,
        out_specs=[hbm] * 5,
        scratch_shapes=scratch,
        compiler_params=pltpu.CompilerParams(
            collective_id=level, has_side_effects=True, vmem_limit_bytes=63 * 1024 * 1024),
        cost_estimate=pl.CostEstimate(flops=18 * CHUNKS * R * W * U, bytes_accessed=10 * 2**20, transcendentals=0),
    )(slots, sums, sort_orders, column_group, row_mask, tokens, cotangent, w_up, w_gate, w_down)


def hand_over(*refs):
    n = len(refs) // 2
    sems = refs[-1]
    copies = [pltpu.make_async_copy(refs[i], refs[n + i], sems.at[i]) for i in range(n)]
    for copy in copies:
        copy.start()
    for copy in copies:
        copy.wait()


def body(tokens, cotangent, block_masks, w_up, w_gate, w_down):
    owners, Y = lax.axis_size("seq"), lax.axis_size("ffn")
    S, Z = PLANE, owners // PLANE
    _, group_len, W = tokens.shape
    groups = block_masks.shape[0]
    U = w_up.shape[1]
    owner_blocks = U // BLK
    quarter = S * CAP * ROWS // Y
    hops = hop_counts(Z)
    my_owner = lax.axis_index("seq")
    z, s = my_owner // S, my_owner % S

    live = block_masks > 0
    need = jnp.any(live.reshape(Z, S, Z, S * owner_blocks), axis=3)
    planes = jnp.arange(Z)
    onward = (planes[None, :] - planes[:, None]) % Z
    reach, rank, order = {}, {}, {}
    group_in_plane = jnp.arange(S, dtype=jnp.int32)
    for direction in range(2):
        distance = onward if direction == 0 else (Z - onward) % Z
        for limit in sorted(set(hops[0])):
            usable = need & (distance <= limit)[:, None, :]
            far = jnp.max(jnp.where(usable, distance[:, None, :], 0), axis=2)
            key = far * S + (S - 1 - group_in_plane)
            place = jnp.sum((key[:, None, :] > key[:, :, None]).astype(jnp.int32), axis=2)
            reach[direction, limit], rank[direction, limit] = far, place
            order[direction, limit] = jnp.sum(
                jnp.where(place[:, None, :] == group_in_plane[None, :, None], group_in_plane[None, None, :], 0), axis=2)

    mine = lax.dynamic_slice_in_dim(live, z * S * owner_blocks, S * owner_blocks, 1)
    active = jnp.any(mine.reshape(groups, S, owner_blocks), axis=2).T
    ordinal = jnp.cumsum(active.astype(jnp.int32), axis=1) - 1
    slot_ids = jnp.arange(CAP, dtype=jnp.int32)
    picked = (ordinal[:, None, :] == slot_ids[None, :, None]) & active[:, None, :]
    group_ids = jnp.arange(groups, dtype=jnp.int32)
    held = jnp.any(picked, axis=2).reshape(-1)
    picked_rows = picked.reshape(S * CAP, groups)

    def look_up(table):
        return jnp.sum(jnp.where(picked_rows, table.reshape(1, groups), 0), axis=1)
    slot_group = look_up(group_ids)
    held_group = jnp.where(held, slot_group, -1)
    away_of = jnp.where(held, (z - slot_group // S) % Z, 0)
    slot_place, sum_orders, sort_orders = [], [], []
    for a in range(2):
        ranks = [look_up(rank[d, hops[a][d]]) for d in range(2)]
        place = jnp.where(away_of <= hops[a][0], ranks[0], ranks[1])
        place = jnp.where(away_of == 0, jnp.where(held, slot_group % S, 0), place)
        slot_place.append((away_of, place))
        sum_orders.append([])
        for d in range(2):
            sort_orders.append(lax.dynamic_index_in_dim(order[d, hops[a][d]], z, 0, keepdims=False))
            row = []
            for far in range(1, hops[a][d] + 1):
                target = (z + far) % Z if d == 0 else (z + Z - far) % Z
                row.append(target * S + lax.dynamic_index_in_dim(order[1 - d, hops[a][d]], target, 0, keepdims=False))
            sum_orders[a].append(row)
    sort_orders = jnp.stack(sort_orders)
    own_groups = z * S + group_in_plane

    my_picked = lax.dynamic_index_in_dim(picked, s, 0, keepdims=False)
    my_columns = lax.dynamic_slice_in_dim(block_masks, my_owner * owner_blocks, owner_blocks, 1)
    block_live = jnp.sum(jnp.where(my_picked[:, :, None], my_columns[None], 0), axis=1).astype(F32)
    unit_live = jnp.repeat(block_live, BLK, axis=1)
    row_mask = jnp.broadcast_to(
        unit_live[None, :, None, :], (quarter // (CAP * ROWS), CAP, ROWS, U)).reshape(quarter, U)

    table = levels(Z, S)
    branches = [functools.partial(ffn, i, caps, Z, S, Y, U) for i, caps in enumerate(table)]
    level = jnp.int32(0)
    for caps in table[:-1]:
        fits = jnp.bool_(True)
        for (direction, limit), far in reach.items():
            for hop in range(1, limit + 1):
                most = jnp.max(jnp.sum((far >= hop).astype(jnp.int32), axis=1))
                fits = fits & (most <= caps[limit][hop - 1])
        level = level + jnp.where(fits, 0, 1)
    arguments = (held_group, slot_place, (own_groups, sum_orders), sort_orders, row_mask,
                 tokens.reshape(group_len, W), cotangent.reshape(group_len, W), w_up, w_gate, w_down)
    results = branches[0](*arguments) if len(table) == 1 else lax.switch(level, branches, *arguments)
    hbm = pl.BlockSpec(memory_space=pl.ANY)
    results = pl.pallas_call(
        hand_over, out_shape=tuple(jax.ShapeDtypeStruct(r.shape, r.dtype) for r in results),
        in_specs=[hbm] * len(results), out_specs=[hbm] * len(results),
        scratch_shapes=[pltpu.SemaphoreType.DMA((len(results),))])(*results)
    outputs, grad_tokens, grad_up, grad_gate, grad_down = results
    return outputs[None], grad_tokens[None], grad_up, grad_gate, grad_down


def solution(mesh):
    in_specs = (
        P("seq", None, "ffn"),
        P("seq", None, "ffn"),
        P(),
        P("ffn", "seq"),
        P("ffn", "seq"),
        P("seq", "ffn"),
    )
    out_specs = (
        P("seq", None, "ffn"),
        P("seq", None, "ffn"),
        P("ffn", "seq"),
        P("ffn", "seq"),
        P("seq", "ffn"),
    )
    return jax.shard_map(body, mesh=mesh, in_specs=in_specs, out_specs=out_specs, check_vma=False)
```

```python
import functools

import jax
import jax.numpy as jnp
from jax import lax
from jax.experimental import pallas as pl
from jax.experimental.pallas import tpu as pltpu
from jax.sharding import PartitionSpec as P

BLK = 128
CAP = 3
PLANE = 8
ROWS = 16
CHUNKS = 2
MESH = pl.DeviceIdType.MESH
F32, BF16 = jnp.float32, jnp.bfloat16


def dot(left, right, dims):
    return lax.dot_general(left, right, (((dims[0],), (dims[1],)), ((), ())), preferred_element_type=F32)


def offsets(caps, hops, S):
    at, table = S, []
    for direction in range(2):
        row = []
        for count in caps[hops[direction]]:
            row.append(at)
            at += count
        table.append(row)
    return table, at


def hop_counts(Z):
    far, near = Z // 2, Z - 1 - Z // 2
    return ((far, near), (near, far))


def kernel(Z, S, Y, W, U, caps, slots, sums, orders, column_group, row_mask, tok, cot, wu_in, wg_in, wd_in,
           out, gtok, gu_out, gg_out, gd_out,
           ag0, ag1, ag2, ag3, so0, so1, so2, so3, pk0, pk1, rw0, rw1, rw2, rw3, wu, wg, wd, part, py0, py1, act0, act1,
           op0, op1, pr0, pr1, pr2, pr3, rs0, rs1, f00, f01, f10, f11, fin0, fin1, fin2, fin3, sel,
           sort0, sort1, sort2, sort3,
           w_sem, sp_send, sp_recv, ag_send, ag_recv, pk_send, rw_recv, y_send, y_recv,
           op_send, pr_recv, rs_send, rs_recv, fin_send, out_recv, g_sem, free):
    ag, pk, rw = (ag0, ag1, ag2, ag3), (pk0, pk1), (rw0, rw1, rw2, rw3)
    py, act = (py0, py1), (act0, act1)
    op, pr = (op0, op1), (pr0, pr1, pr2, pr3)
    rs, first, fin = (rs0, rs1), ((f00, f01), (f10, f11)), (fin0, fin1, fin2, fin3)
    sorted_rows, sort = ((so0, so1), (so2, so3)), ((sort0, sort1), (sort2, sort3))
    sources, results = (tok, cot), (out, gtok)
    R = S * CAP * ROWS
    SLICE = CHUNKS * ROWS
    seq, y = lax.axis_index("seq"), lax.axis_index("ffn")
    z, s = seq // S, seq % S
    up_z, down_z = lax.rem(z + 1, Z), lax.rem(z + Z - 1, Z)
    toward = (up_z, down_z)
    hops = hop_counts(Z)
    blocks = [offsets(caps, hops[a], S)[0] for a in range(2)]

    def mate(d):
        return lax.rem(s + d, S)

    def in_plane(t):
        return (z * S + t, y)

    def along_z(direction):
        return (toward[direction] * S + s, y)

    def across_y(d):
        return (seq, lax.rem(y + d, Y))

    def each_mate(fn):
        def step(d, carry):
            fn(mate(d))
            return carry
        lax.fori_loop(1, S, step, 0)

    def settle(ref, sem):
        pltpu.make_async_copy(ref, ref, sem).wait()

    def spread(u):
        source, k = sources[u % 2], u // 2

        def piece(t):
            return source.at[pl.ds(pl.multiple_of(t * SLICE + k * ROWS, ROWS), ROWS)]

        def go(t):
            pltpu.make_async_remote_copy(
                src_ref=piece(t), dst_ref=ag[u].at[s], send_sem=sp_send.at[u], recv_sem=sp_recv.at[u],
                device_id=in_plane(t), device_id_type=MESH).start()
        each_mate(go)
        pltpu.make_async_copy(piece(s), ag[u].at[s], sp_recv.at[u]).start()

    def arrivals(a, direction, hop, count):
        return pl.ds(blocks[a][direction][hop - 1], count)

    def ag_copy(u, half, direction, hop):
        a, columns = u % 2, half_of(half)
        count = caps[hops[a][direction]][hop - 1]
        if hop == 1:
            source = sorted_rows[a][direction].at[:, :, columns]
        else:
            source = ag[u].at[arrivals(a, direction, hop - 1, count), :, columns]
        return pltpu.make_async_remote_copy(
            src_ref=source, dst_ref=ag[u].at[arrivals(a, direction, hop, count), :, columns],
            send_sem=ag_send.at[u, half, direction, hop - 1], recv_sem=ag_recv.at[u, half, direction, hop - 1],
            device_id=along_z(direction), device_id_type=MESH)

    def ag_start(u):
        a = u % 2
        settle(ag[u].at[pl.ds(0, S)], sp_recv.at[u])
        for half in range(2):
            for direction in range(2):
                target = sorted_rows[a][direction]
                if u >= 2:
                    ag_copy(u - 2, half, direction, 1).wait_send()

                def step(columns):
                    own = ag[u][0:S, :, columns].reshape(S * ROWS, columns.size)
                    moved = dot(sort[a][direction][...], own, (1, 0)).astype(BF16)
                    target[:, :, columns] = moved.reshape(target.shape[0], ROWS, columns.size)
                half_loop(half, step)
                ag_copy(u, half, direction, 1).start()

    def ag_forward(u, hop, half):
        for direction in range(2):
            if hop <= hops[u % 2][direction]:
                ag_copy(u, half, direction, hop - 1).wait_recv()
                ag_copy(u, half, direction, hop).start()

    def ag_finish(u):
        for half in range(2):
            for direction in range(2):
                ag_copy(u, half, direction, hops[u % 2][direction]).wait_recv()

    def pack(u):
        a = u % 2
        if u >= 2:
            settle(pk[a].at[pl.ds(0, S - 1)], pk_send.at[u - 2])

        def go(t):
            for j in range(CAP):
                pk[a][t, j] = ag[u][slots[a, t * CAP + j]]
            pltpu.make_async_remote_copy(
                src_ref=pk[a].at[t], dst_ref=rw[u].at[s], send_sem=pk_send.at[u], recv_sem=rw_recv.at[u],
                device_id=in_plane(t), device_id_type=MESH).start()
        each_mate(go)
        for j in range(CAP):
            rw[u][s, j] = ag[u][slots[a, s * CAP + j]]

    def rows_ready(u):
        settle(rw[u].at[pl.ds(0, S - 1)], rw_recv.at[u])

    def feature_loop(width, fn):
        def step(b, carry):
            fn(pl.ds(pl.multiple_of(b * width, width), width))
            return carry
        lax.fori_loop(0, W // width, step, 0)

    HALF = W // 2
    piece_width = min(512, HALF)

    def half_of(half):
        return pl.ds(half * HALF, HALF)

    def half_loop(half, fn):
        def step(b, carry):
            fn(pl.ds(pl.multiple_of(half * HALF + b * piece_width, piece_width), piece_width))
            return carry
        lax.fori_loop(0, HALF // piece_width, step, 0)

    def wide(ref, columns):
        return ref[:, :, :, columns].reshape(R, columns.size)

    def split(rows):
        return rows.reshape(Y, R // Y, U)

    def up_and_gate(k):
        if k:
            settle(part.at[pl.ds(0, Y - 1)], y_send.at[k - 1, 0])
        part[...] = jnp.zeros_like(part)

        def step(columns):
            x = wide(rw[2 * k], columns)
            part[:, 0] += split(dot(x, wu[columns, :], (1, 0)))
            part[:, 1] += split(dot(x, wg[columns, :], (1, 0)))
        feature_loop(min(512, W), step)

    def hidden_grad(k):
        def step(columns):
            x = wide(rw[2 * k + 1], columns)
            part[:, 2] += split(dot(x, wd[:, columns], (1, 1)))
        feature_loop(min(512, W), step)

    def sum_send(k):
        for d in range(1, Y):
            pltpu.make_async_remote_copy(
                src_ref=part.at[lax.rem(y + d, Y)], dst_ref=py[k].at[d - 1], send_sem=y_send.at[k, 0],
                recv_sem=y_recv.at[k, 0], device_id=across_y(d), device_id_type=MESH).start()

    def activate(k):
        settle(py[k], y_recv.at[k, 0])
        total = [part[y, i] for i in range(3)]
        for d in range(Y - 1):
            total = [total[i] + py[k][d, i] for i in range(3)]
        mask = row_mask[...]
        rectified = jnp.maximum(total[1], 0.0)
        square = rectified * rectified
        grad = total[2] * mask
        act[k][y, 0] = (square * total[0] * mask).astype(BF16)
        act[k][y, 1] = (grad * square).astype(BF16)
        act[k][y, 2] = (grad * total[0] * 2.0 * rectified).astype(BF16)
        for d in range(1, Y):
            pltpu.make_async_remote_copy(
                src_ref=act[k].at[y], dst_ref=act[k].at[y], send_sem=y_send.at[k, 1],
                recv_sem=y_recv.at[k, 1], device_id=across_y(d), device_id_type=MESH).start()

    def act_ready(k):
        settle(act[k].at[pl.ds(0, Y - 1)], y_recv.at[k, 1])

    def activation(k, i):
        return act[k][:, i].reshape(R, U)

    def give_back(u):
        a = u % 2

        def go(t):
            pltpu.make_async_remote_copy(
                src_ref=op[a].at[t], dst_ref=pr[u].at[s], send_sem=op_send.at[u], recv_sem=pr_recv.at[u],
                device_id=in_plane(t), device_id_type=MESH).start()
        each_mate(go)
        pltpu.make_async_copy(op[a].at[s], pr[u].at[s], pr_recv.at[u]).start()

    def down(k):
        u = 2 * k
        if k:
            settle(op[0].at[pl.ds(0, S - 1)], op_send.at[u - 2])

        def step(columns):
            product = dot(activation(k, 0), wd[:, columns], (1, 0))
            op[0][:, :, :, columns] = product.astype(BF16).reshape(S, CAP, ROWS, columns.size)
        feature_loop(min(512, W), step)
        give_back(u)

    def back(k):
        u = 2 * k + 1
        if k:
            settle(op[1].at[pl.ds(0, S - 1)], op_send.at[u - 2])

        def step(columns):
            product = dot(activation(k, 1), wu[columns, :], (1, 1))
            product = product + dot(activation(k, 2), wg[columns, :], (1, 1))
            op[1][:, :, :, columns] = product.astype(BF16).reshape(S, CAP, ROWS, columns.size)
        feature_loop(min(512, W), step)
        give_back(u)

    def collected(u):
        settle(pr[u], pr_recv.at[u])

    sum_rows = [S * ROWS]
    sum_at = []
    for a in range(2):
        sum_at.append([])
        for direction in range(2):
            row = []
            for count in caps[hops[a][direction]]:
                row.append(sum_rows[0])
                sum_rows[0] += count * ROWS
            sum_at[a].append(row)

    def plane_sum(u, direction, far, columns):
        a = u % 2
        at, count = (0, S) if far == 0 else (sum_at[a][direction][far - 1], caps[hops[a][direction]][far - 1])
        pick = sel[at:at + count * ROWS, :]
        return dot(pick, wide(pr[u], columns), (1, 0)).reshape(count, ROWS, columns.size)

    room = []
    for a in range(2):
        at, table = 0, []
        for direction in range(2):
            row, counts = [], caps[hops[a][direction]]
            for hop in range(1, len(counts) + 1):
                row.append(at)
                at += counts[max(len(counts) - hop, 1) - 1]
            table.append(row)
        room.append(table)

    def received(a, direction, hop, count):
        return rs[a].at[pl.ds(room[a][direction][hop - 1], count)]

    def rs_copy(u, half, direction, hop):
        a, columns = u % 2, half_of(half)
        counts = caps[hops[a][direction]]
        count = counts[len(counts) - hop]
        if hop == 1:
            source = first[a][direction].at[:, :, columns]
        else:
            source = received(a, direction, hop - 1, count).at[:, :, columns]
        return pltpu.make_async_remote_copy(
            src_ref=source, dst_ref=received(a, direction, hop, count).at[:, :, columns],
            send_sem=rs_send.at[u, half, direction, hop - 1], recv_sem=rs_recv.at[u, half, direction, hop - 1],
            device_id=along_z(direction), device_id_type=MESH)

    def release(u, half, direction):
        if u < 2:
            pl.semaphore_signal(
                free.at[u, half, direction], inc=1, device_id=along_z(1 - direction), device_id_type=MESH)

    def rs_step(u, half, direction, hop):
        a = u % 2
        last = hops[a][direction]
        if hop > last:
            return
        far = last - hop + 1
        if hop == 1:
            if u >= 2:
                rs_copy(u - 2, half, direction, 1).wait_send()

            def step(columns):
                first[a][direction][:, :, columns] = plane_sum(u, direction, far, columns).astype(BF16)
        else:
            if hop > 2:
                rs_copy(u, half, direction, hop - 1).wait_send()
                release(u, half, direction)
            rs_copy(u, half, direction, hop - 1).wait_recv()
            old = caps[last][far]
            arrived = received(a, direction, hop - 1, old)
            fresh = rs[a].at[pl.ds(room[a][direction][hop - 2] + old, caps[last][far - 1] - old)]

            def step(columns):
                total = plane_sum(u, direction, far, columns)
                arrived[:, :, columns] = (arrived[:, :, columns].astype(F32) + total[:old]).astype(BF16)
                if caps[last][far - 1] > old:
                    fresh[:, :, columns] = total[old:].astype(BF16)
        half_loop(half, step)
        if u >= 2:
            pl.semaphore_wait(free.at[u - 2, half, direction], 1)
        rs_copy(u, half, direction, hop).start()

    def rs_both(u, hop, half):
        for direction in range(2):
            rs_step(u, half, direction, hop)

    def rs_start(u):
        collected(u)
        for half in range(2):
            rs_both(u, 1, half)

    def finish(u):
        a, k = u % 2, u // 2
        for half in range(2):
            ends = []
            for direction in range(2):
                last = hops[a][direction]
                if last > 1:
                    rs_copy(u, half, direction, last).wait_send()
                    release(u, half, direction)
                rs_copy(u, half, direction, last).wait_recv()
                ends.append(received(a, direction, last, caps[last][0]))

            def step(columns):
                total = plane_sum(u, 0, 0, columns)
                for direction in range(2):
                    arrived = ends[direction][:, :, columns].reshape(-1, columns.size)
                    total = total + dot(sort[1 - a][1 - direction][...], arrived, (0, 0)).reshape(
                        S, ROWS, columns.size)
                fin[u][:, :, columns] = total.astype(BF16)
            half_loop(half, step)
            for direction in range(2):
                release(u, half, direction)
        place = results[a].at[pl.ds(pl.multiple_of(s * SLICE + k * ROWS, ROWS), ROWS)]

        def go(t):
            pltpu.make_async_remote_copy(
                src_ref=fin[u].at[t], dst_ref=place, send_sem=fin_send.at[u], recv_sem=out_recv.at[u],
                device_id=in_plane(t), device_id_type=MESH).start()
        each_mate(go)
        pltpu.make_async_copy(fin[u].at[s], place, out_recv.at[u]).start()

    def token_weight_grad(i, buffer, target):
        width = min(256, W)

        def step(b, carry):
            columns = pl.ds(pl.multiple_of(b * width, width), width)
            total = dot(wide(rw[0], columns), activation(0, i), (0, 0))
            total = total + dot(wide(rw[2], columns), activation(1, i), (0, 0))
            buffer[columns, :] = (total * grad_scale).astype(BF16)
            return carry
        lax.fori_loop(0, W // width, step, 0)
        pltpu.make_async_copy(buffer, target, g_sem.at[i]).start()

    def down_weight_grad(buffer, target):
        width = min(256, W)

        def step(columns):
            total = dot(activation(0, 0), wide(rw[1], columns), (0, 0))
            total = total + dot(activation(1, 0), wide(rw[3], columns), (0, 0))
            buffer[:, columns] = (total * grad_scale).astype(BF16)
        feature_loop(width, step)
        pltpu.make_async_copy(buffer, target, g_sem.at[0]).start()

    grad_scale = 1.0 / (S * SLICE)
    weights = [pltpu.make_async_copy(wu_in, wu, w_sem.at[0]), pltpu.make_async_copy(wg_in, wg, w_sem.at[1]),
               pltpu.make_async_copy(wd_in, wd, w_sem.at[2])]
    for copy in weights:
        copy.start()

    barrier = pltpu.get_barrier_semaphore()

    def greet(device):
        pl.semaphore_signal(barrier, inc=1, device_id=device, device_id_type=MESH)
    each_mate(lambda t: greet(in_plane(t)))
    for direction in range(2):
        greet(along_z(direction))
    for d in range(1, Y):
        greet(across_y(d))
    pl.semaphore_wait(barrier, S - 1 + 2 + Y - 1)

    spread(0)
    for a in range(2):
        for direction in range(2):
            for r in range(caps[hops[a][direction]][0]):
                row = lax.broadcasted_iota(jnp.int32, (ROWS, S * ROWS), 0)
                column = lax.broadcasted_iota(jnp.int32, (ROWS, S * ROWS), 1)
                hit = column == orders[2 * a + direction, r] * ROWS + row
                sort[a][direction][r * ROWS:(r + 1) * ROWS, :] = jnp.where(hit, 1.0, 0.0).astype(BF16)
    ag_start(0)
    spread(1)

    def select_rows(g, carry):
        row = lax.broadcasted_iota(jnp.int32, (ROWS, R), 0)
        column = lax.broadcasted_iota(jnp.int32, (ROWS, R), 1)
        hit = (column_group[...] == sums[g]) & (lax.rem(column, ROWS) == row)
        sel[pl.ds(pl.multiple_of(g * ROWS, ROWS), ROWS), :] = jnp.where(hit, 1.0, 0.0).astype(BF16)
        return carry
    lax.fori_loop(0, sum_rows[0] // ROWS, select_rows, 0)
    for copy in weights:
        copy.wait()

    far = max(hops[0])

    def run(step, u, pieces):
        events = [(hop, half) for hop in range(2, far + 1) for half in range(2)]
        for fn in pieces.get(0, ()):
            fn()
        for i, (hop, half) in enumerate(events):
            step(u, hop, half)
            for fn in pieces.get(i + 1, ()):
                fn()
        for i in range(len(events) + 1, 8):
            for fn in pieces.get(i, ()):
                fn()

    def each(*fns):
        return tuple(functools.partial(*fn) for fn in fns)

    run(ag_forward, 0, {2: each((ag_start, 1), (spread, 2))})
    run(ag_forward, 1, {
        0: each((ag_finish, 0), (pack, 0)),
        2: each((ag_start, 2), (spread, 3)),
        5: each((rows_ready, 0), (up_and_gate, 0))})
    run(ag_forward, 2, {
        0: each((ag_finish, 1), (pack, 1)),
        2: each((ag_start, 3)),
        5: each((rows_ready, 1), (hidden_grad, 0), (sum_send, 0))})
    run(ag_forward, 3, {
        0: each((ag_finish, 2), (pack, 2)),
        1: each((activate, 0)),
        3: each((act_ready, 0), (down, 0)),
        6: each((rows_ready, 2), (up_and_gate, 1), (ag_finish, 3), (pack, 3))})
    rs_start(0)
    run(rs_both, 0, {
        0: each((back, 0)),
        5: each((rows_ready, 3), (hidden_grad, 1), (sum_send, 1)),
        6: each((rs_start, 1), (activate, 1))})
    run(rs_both, 1, {
        0: each((finish, 0)),
        1: each((act_ready, 1), (down, 1)),
        4: each((back, 1)),
        6: each((rs_start, 2))})
    run(rs_both, 2, {
        0: each((finish, 1)),
        2: each((token_weight_grad, 1, wu, gu_out)),
        4: each((token_weight_grad, 2, wg, gg_out)),
        6: each((rs_start, 3))})
    run(rs_both, 3, {
        0: each((finish, 2)),
        2: each((down_weight_grad, wd, gd_out))})
    finish(3)

    for u in range(4):
        a, k = u % 2, u // 2
        settle(sources[a].at[pl.ds(0, (S - 1) * ROWS)], sp_send.at[u])
        for half in range(2):
            for direction in range(2):
                for hop in range(1 if k else 2, hops[a][direction] + 1):
                    ag_copy(u, half, direction, hop).wait_send()
        settle(fin[u].at[pl.ds(0, S - 1)], fin_send.at[u])
        settle(results[a].at[pl.ds(0, S * ROWS)], out_recv.at[u])
    for u in (2, 3):
        a = u % 2
        settle(pk[a].at[pl.ds(0, S - 1)], pk_send.at[u])
        settle(op[a].at[pl.ds(0, S - 1)], op_send.at[u])
        for half in range(2):
            for direction in range(2):
                rs_copy(u, half, direction, 1).wait_send()
    settle(part.at[pl.ds(0, Y - 1)], y_send.at[1, 0])
    for k in range(CHUNKS):
        settle(act[k].at[pl.ds(0, Y - 1)], y_send.at[k, 1])
    for i, (buffer, target) in enumerate(((wd, gd_out), (wu, gu_out), (wg, gg_out))):
        pltpu.make_async_copy(buffer, target, g_sem.at[i]).wait()


def levels(Z, S):
    far = Z // 2
    full = {far: (S,) * far, Z - 1 - far: (S,) * (Z - 1 - far)}
    if (Z, S) != (8, 8):
        return [full]
    return [{4: (7, 6, 5, 3), 3: (6, 5, 4)}, {4: (8, 7, 6, 4), 3: (7, 6, 4)}, full]


def ffn(level, caps, Z, S, Y, U, held_group, slot_place, sum_orders, sort_orders, row_mask, tokens, cotangent,
        w_up, w_gate, w_down):
    group_len, W = tokens.shape
    R = S * CAP * ROWS
    quarter = R // Y
    hops = hop_counts(Z)
    start = [offsets(caps, hops[a], S) for a in range(2)]
    slots = []
    for a in range(2):
        away, rank = slot_place[a]
        first = jnp.asarray([0] + start[a][0][0] + start[a][0][1][::-1], jnp.int32)
        slots.append(jnp.sum(jnp.where(away[:, None] == jnp.arange(Z)[None, :], first[None, :], 0), axis=1) + rank)
    slots = jnp.stack(slots).astype(jnp.int32)
    sums = [sum_orders[0]]
    for a in range(2):
        for direction in range(2):
            for far, count in enumerate(caps[hops[a][direction]]):
                sums.append(sum_orders[1][a][direction][far][:count])
    sums = jnp.concatenate(sums).astype(jnp.int32)
    column_group = jnp.repeat(held_group, ROWS).reshape(1, R)

    hbm, vmem = pl.BlockSpec(memory_space=pl.ANY), pl.BlockSpec(memory_space=pltpu.VMEM)
    smem = pl.BlockSpec(memory_space=pltpu.SMEM)
    half = Z // 2
    rows = pltpu.VMEM((S, CAP, ROWS, W), BF16)
    dma = pltpu.SemaphoreType.DMA

    def groups_of(count):
        return pltpu.VMEM((count, ROWS, W), BF16)

    def counts(a, direction):
        return caps[hops[a][direction]]
    ways = [(a, direction) for a in range(2) for direction in range(2)]
    room = [sum(sum(counts(a, d)[max(len(counts(a, d)) - hop, 1) - 1] for hop in range(1, len(counts(a, d)) + 1))
                for d in range(2)) for a in range(2)]
    scratch = (
        [groups_of(start[u % 2][1]) for u in range(4)]
        + [groups_of(counts(a, d)[0]) for a, d in ways]
        + [rows] * 2 + [rows] * 4
        + [pltpu.VMEM((W, U), BF16)] * 2 + [pltpu.VMEM((U, W), BF16)]
        + [pltpu.VMEM((Y, 3, quarter, U), F32)]
        + [pltpu.VMEM((Y - 1, 3, quarter, U), F32)] * 2
        + [pltpu.VMEM((Y, 3, quarter, U), BF16)] * 2
        + [rows] * 2 + [rows] * 4
        + [groups_of(room[a]) for a in range(2)]
        + [groups_of(counts(a, d)[-1]) for a, d in ways]
        + [groups_of(S)] * 4
        + [pltpu.VMEM((sums.shape[0] * ROWS, R), BF16)]
        + [pltpu.VMEM((counts(a, d)[0] * ROWS, S * ROWS), BF16) for a, d in ways]
        + [
            dma((3,)), dma((4,)), dma((4,)), dma((4, 2, 2, half)), dma((4, 2, 2, half)), dma((4,)), dma((4,)),
            dma((2, 2)), dma((2, 2)), dma((4,)), dma((4,)), dma((4, 2, 2, half)), dma((4, 2, 2, half)), dma((4,)),
            dma((4,)), dma((3,)), pltpu.SemaphoreType.REGULAR((2, 2, 2)),
        ]
    )
    shapes = (
        jax.ShapeDtypeStruct((group_len, W), BF16), jax.ShapeDtypeStruct((group_len, W), BF16),
        jax.ShapeDtypeStruct((W, U), BF16), jax.ShapeDtypeStruct((W, U), BF16), jax.ShapeDtypeStruct((U, W), BF16),
    )
    return pl.pallas_call(
        functools.partial(kernel, Z, S, Y, W, U, caps),
        out_shape=shapes,
        in_specs=[smem] * 3 + [vmem] * 2 + [hbm] * 5,
        out_specs=[hbm] * 5,
        scratch_shapes=scratch,
        compiler_params=pltpu.CompilerParams(
            collective_id=level, has_side_effects=True, vmem_limit_bytes=63 * 1024 * 1024),
        cost_estimate=pl.CostEstimate(flops=18 * CHUNKS * R * W * U, bytes_accessed=10 * 2**20, transcendentals=0),
    )(slots, sums, sort_orders, column_group, row_mask, tokens, cotangent, w_up, w_gate, w_down)


def hand_over(*refs):
    n = len(refs) // 2
    for i in range(n):
        refs[n + i][...] = refs[i][...]


def body(tokens, cotangent, block_masks, w_up, w_gate, w_down):
    owners, Y = lax.axis_size("seq"), lax.axis_size("ffn")
    S, Z = PLANE, owners // PLANE
    _, group_len, W = tokens.shape
    groups = block_masks.shape[0]
    U = w_up.shape[1]
    owner_blocks = U // BLK
    quarter = S * CAP * ROWS // Y
    hops = hop_counts(Z)
    my_owner = lax.axis_index("seq")
    z, s = my_owner // S, my_owner % S

    live = block_masks > 0
    need = jnp.any(live.reshape(Z, S, Z, S * owner_blocks), axis=3)
    planes = jnp.arange(Z)
    onward = (planes[None, :] - planes[:, None]) % Z
    group_in_plane = jnp.arange(S, dtype=jnp.int32)
    limits = sorted(set(hops[0]))
    keys = [(direction, limit) for direction in range(2) for limit in limits]
    distance = jnp.stack([onward if direction == 0 else (Z - onward) % Z for direction, _ in keys])
    limit_of = jnp.asarray([limit for _, limit in keys])[:, None, None]
    distance = jnp.where(distance <= limit_of, distance, 0).astype(jnp.int32)
    reach = jnp.max(jnp.where(need[None], distance[:, :, None, :], 0), axis=3)
    key = reach * S + (S - 1 - group_in_plane)
    rank = jnp.sum((key[:, :, None, :] > key[:, :, :, None]).astype(jnp.int32), axis=3)
    order = jnp.sum(
        jnp.where(rank[:, :, None, :] == group_in_plane[:, None], group_in_plane, 0), axis=3)

    mine = lax.dynamic_slice_in_dim(live, z * S * owner_blocks, S * owner_blocks, 1)
    active = jnp.any(mine.reshape(groups, S, owner_blocks), axis=2).T
    ordinal = jnp.cumsum(active.astype(jnp.int32), axis=1) - 1
    slot_ids = jnp.arange(CAP, dtype=jnp.int32)
    picked = (ordinal[:, None, :] == slot_ids[None, :, None]) & active[:, None, :]
    group_ids = jnp.arange(groups, dtype=jnp.int32)
    held = jnp.any(picked, axis=2).reshape(-1)
    picked_rows = picked.reshape(S * CAP, groups)

    def look_up(table):
        return jnp.sum(jnp.where(picked_rows, table.reshape(1, groups), 0), axis=1)
    slot_group = look_up(group_ids)
    held_group = jnp.where(held, slot_group, -1)
    away_of = jnp.where(held, (z - slot_group // S) % Z, 0)
    slot_place, sum_orders, sort_orders = [], [], []
    for a in range(2):
        ranks = [look_up(rank[keys.index((d, hops[a][d]))]) for d in range(2)]
        place = jnp.where(away_of <= hops[a][0], ranks[0], ranks[1])
        place = jnp.where(away_of == 0, jnp.where(held, slot_group % S, 0), place)
        slot_place.append((away_of, place))
        sum_orders.append([])
        for d in range(2):
            sort_orders.append(lax.dynamic_index_in_dim(order[keys.index((d, hops[a][d]))], z, 0, keepdims=False))
            row = []
            for far in range(1, hops[a][d] + 1):
                target = (z + far) % Z if d == 0 else (z + Z - far) % Z
                row.append(target * S + lax.dynamic_index_in_dim(order[keys.index((1 - d, hops[a][d]))], target, 0, keepdims=False))
            sum_orders[a].append(row)
    sort_orders = jnp.stack(sort_orders)
    own_groups = z * S + group_in_plane

    my_picked = lax.dynamic_index_in_dim(picked, s, 0, keepdims=False)
    my_columns = lax.dynamic_slice_in_dim(block_masks, my_owner * owner_blocks, owner_blocks, 1)
    block_live = jnp.sum(jnp.where(my_picked[:, :, None], my_columns[None], 0), axis=1).astype(F32)
    unit_live = jnp.repeat(block_live, BLK, axis=1)
    row_mask = jnp.broadcast_to(
        unit_live[None, :, None, :], (quarter // (CAP * ROWS), CAP, ROWS, U)).reshape(quarter, U)

    table = levels(Z, S)
    branches = [functools.partial(ffn, i, caps, Z, S, Y, U) for i, caps in enumerate(table)]
    far = max(limits)
    steps = jnp.arange(1, far + 1)[None, None, :, None]
    most = jnp.max(jnp.sum((reach[:, :, None, :] >= steps).astype(jnp.int32), axis=3), axis=1)
    allowed = [[list(caps[limit]) + [0] * (far - limit) for _, limit in keys] for caps in table]
    level = jnp.sum(jnp.any(most[None] > jnp.asarray(allowed[:-1], jnp.int32).reshape(-1, len(keys), far),
                            axis=(1, 2)).astype(jnp.int32))
    arguments = (held_group, slot_place, (own_groups, sum_orders), sort_orders, row_mask,
                 tokens.reshape(group_len, W), cotangent.reshape(group_len, W), w_up, w_gate, w_down)
    results = branches[0](*arguments) if len(table) == 1 else lax.switch(level, branches, *arguments)
    parts = 8
    specs = [pl.BlockSpec((r.shape[0] // parts, r.shape[1]), lambda i: (i, 0)) for r in results]
    results = pl.pallas_call(
        hand_over, out_shape=tuple(jax.ShapeDtypeStruct(r.shape, r.dtype) for r in results), grid=(parts,),
        in_specs=specs, out_specs=specs)(*results)
    outputs, grad_tokens, grad_up, grad_gate, grad_down = results
    return outputs[None], grad_tokens[None], grad_up, grad_gate, grad_down


def solution(mesh):
    in_specs = (
        P("seq", None, "ffn"),
        P("seq", None, "ffn"),
        P(),
        P("ffn", "seq"),
        P("ffn", "seq"),
        P("seq", "ffn"),
    )
    out_specs = (
        P("seq", None, "ffn"),
        P("seq", None, "ffn"),
        P("ffn", "seq"),
        P("ffn", "seq"),
        P("seq", "ffn"),
    )
    return jax.shard_map(body, mesh=mesh, in_specs=in_specs, out_specs=out_specs, check_vma=False)
```

```python
import functools

import jax
import jax.numpy as jnp
from jax import lax
from jax.experimental import pallas as pl
from jax.experimental.pallas import tpu as pltpu
from jax.sharding import PartitionSpec as P

BLK = 128
CAP = 3
PLANE = 8
ROWS = 16
CHUNKS = 2
MESH = pl.DeviceIdType.MESH
F32, BF16 = jnp.float32, jnp.bfloat16


def dot(left, right, dims):
    return lax.dot_general(left, right, (((dims[0],), (dims[1],)), ((), ())), preferred_element_type=F32)


def offsets(caps, hops, S):
    at, table = S, []
    for direction in range(2):
        row = []
        for count in caps[hops[direction]]:
            row.append(at)
            at += count
        table.append(row)
    return table, at


def hop_counts(Z):
    far, near = Z // 2, Z - 1 - Z // 2
    return ((far, near), (near, far))


def kernel(Z, S, Y, W, U, caps, slots, sums, orders, column_group, row_mask, tok, cot, wu_in, wg_in, wd_in,
           out, gtok, gu_out, gg_out, gd_out,
           *refs):
    refs = list(refs)

    def take(*shape):
        if not shape:
            return refs.pop(0)
        return [take(*shape[1:]) for _ in range(shape[0])]
    ag, sorted_rows, pk, rw = take(4), take(2, 2, 2), take(2), take(4)
    wu, wg, wd, part = take(4)
    py, act, op, pr, rs, first, fin = take(2), take(2), take(2), take(4), take(2), take(2, 2, 2), take(4)
    sel, sort = take(), take(2, 2)
    (w_sem, sp_send, sp_recv, ag_send, ag_recv, pk_send, rw_recv, y_send, y_recv,
     op_send, pr_recv, rs_send, rs_recv, fin_send, out_recv, g_sem, free) = take(17)
    sources, results = (tok, cot), (out, gtok)
    R = S * CAP * ROWS
    SLICE = CHUNKS * ROWS
    seq, y = lax.axis_index("seq"), lax.axis_index("ffn")
    z, s = seq // S, seq % S
    up_z, down_z = lax.rem(z + 1, Z), lax.rem(z + Z - 1, Z)
    toward = (up_z, down_z)
    hops = hop_counts(Z)
    blocks = [offsets(caps, hops[half], S)[0] for half in range(2)]

    def mate(d):
        return lax.rem(s + d, S)

    def in_plane(t):
        return (z * S + t, y)

    def along_z(direction):
        return (toward[direction] * S + s, y)

    def across_y(d):
        return (seq, lax.rem(y + d, Y))

    def each_mate(fn):
        def step(d, carry):
            fn(mate(d))
            return carry
        lax.fori_loop(1, S, step, 0)

    pending = {}

    def settle(ref, sem):
        pltpu.make_async_copy(ref, ref, sem).wait()

    def expect(key, *wait):
        pending[key] = functools.partial(*wait)

    def await_(*key):
        pending.pop(key)()

    def spread(u):
        source, k = sources[u % 2], u // 2

        def piece(t):
            return source.at[pl.ds(pl.multiple_of(t * SLICE + k * ROWS, ROWS), ROWS)]

        def go(t):
            pltpu.make_async_remote_copy(
                src_ref=piece(t), dst_ref=ag[u].at[s], send_sem=sp_send.at[u], recv_sem=sp_recv.at[u],
                device_id=in_plane(t), device_id_type=MESH).start()
        each_mate(go)
        pltpu.make_async_copy(piece(s), ag[u].at[s], sp_recv.at[u]).start()
        expect(("spread out", u), settle, source.at[pl.ds(0, (S - 1) * ROWS)], sp_send.at[u])
        expect(("spread in", u), settle, ag[u].at[pl.ds(0, S)], sp_recv.at[u])

    def arrivals(half, direction, hop, count):
        return pl.ds(blocks[half][direction][hop - 1], count)

    def ag_copy(u, half, direction, hop):
        columns = half_of(half)
        count = caps[hops[half][direction]][hop - 1]
        if hop == 1:
            source = sorted_rows[u % 2][half][direction]
        else:
            source = ag[u].at[arrivals(half, direction, hop - 1, count), :, columns]
        return pltpu.make_async_remote_copy(
            src_ref=source, dst_ref=ag[u].at[arrivals(half, direction, hop, count), :, columns],
            send_sem=ag_send.at[u, half, direction, hop - 1], recv_sem=ag_recv.at[u, half, direction, hop - 1],
            device_id=along_z(direction), device_id_type=MESH)

    def ag_start(u):
        a = u % 2
        await_("spread in", u)
        for half in range(2):
            for direction in range(2):
                target = sorted_rows[a][half][direction]
                if u >= 2:
                    await_("gather out", u - 2, half, direction, 1)

                def step(columns, local):
                    own = ag[u][0:S, :, columns].reshape(S * ROWS, columns.size)
                    moved = dot(sort[half][direction][...], own, (1, 0)).astype(BF16)
                    target[:, :, local] = moved.reshape(target.shape[0], ROWS, columns.size)
                half_loop(half, step)
                ag_send_on(u, half, direction, 1)

    def ag_send_on(u, half, direction, hop):
        copy = ag_copy(u, half, direction, hop)
        copy.start()
        expect(("gather out", u, half, direction, hop), copy.wait_send)
        expect(("gather in", u, half, direction, hop), copy.wait_recv)

    def ag_forward(u, hop, half):
        for direction in range(2):
            if hop <= hops[half][direction]:
                await_("gather in", u, half, direction, hop - 1)
                ag_send_on(u, half, direction, hop)

    def ag_finish(u):
        for half in range(2):
            for direction in range(2):
                await_("gather in", u, half, direction, hops[half][direction])

    def pack(u):
        a = u % 2
        if u >= 2:
            await_("rows out", u - 2)

        def go(t):
            for j in range(CAP):
                for half in range(2):
                    columns = half_of(half)
                    pk[a][t, j, :, columns] = ag[u][slots[half, t * CAP + j], :, columns]
            pltpu.make_async_remote_copy(
                src_ref=pk[a].at[t], dst_ref=rw[u].at[s], send_sem=pk_send.at[u], recv_sem=rw_recv.at[u],
                device_id=in_plane(t), device_id_type=MESH).start()
        each_mate(go)
        for j in range(CAP):
            for half in range(2):
                columns = half_of(half)
                rw[u][s, j, :, columns] = ag[u][slots[half, s * CAP + j], :, columns]
        expect(("rows out", u), settle, pk[a].at[pl.ds(0, S - 1)], pk_send.at[u])
        expect(("rows in", u), settle, rw[u].at[pl.ds(0, S - 1)], rw_recv.at[u])

    def rows_ready(u):
        await_("rows in", u)

    def feature_loop(width, fn):
        def step(b, carry):
            fn(pl.ds(pl.multiple_of(b * width, width), width))
            return carry
        lax.fori_loop(0, W // width, step, 0)

    HALF = W // 2
    piece_width = min(512, HALF)

    def half_of(half):
        return pl.ds(half * HALF, HALF)

    def half_loop(half, fn):
        def step(b, carry):
            local = pl.multiple_of(b * piece_width, piece_width)
            fn(pl.ds(pl.multiple_of(half * HALF + local, piece_width), piece_width), pl.ds(local, piece_width))
            return carry
        lax.fori_loop(0, HALF // piece_width, step, 0)

    def wide(ref, columns):
        return ref[:, :, :, columns].reshape(R, columns.size)

    def split(rows):
        return rows.reshape(Y, R // Y, U)

    def up_and_gate(k):
        if k:
            await_("sums out", k - 1)
        part[...] = jnp.zeros_like(part)

        def step(columns):
            x = wide(rw[2 * k], columns)
            part[:, 0] += split(dot(x, wu[columns, :], (1, 0)))
            part[:, 1] += split(dot(x, wg[columns, :], (1, 0)))
        feature_loop(min(512, W), step)

    def hidden_grad(k):
        def step(columns):
            x = wide(rw[2 * k + 1], columns)
            part[:, 2] += split(dot(x, wd[:, columns], (1, 1)))
        feature_loop(min(512, W), step)

    def sum_send(k):
        for d in range(1, Y):
            pltpu.make_async_remote_copy(
                src_ref=part.at[lax.rem(y + d, Y)], dst_ref=py[k].at[d - 1], send_sem=y_send.at[k, 0],
                recv_sem=y_recv.at[k, 0], device_id=across_y(d), device_id_type=MESH).start()
        expect(("sums out", k), settle, part.at[pl.ds(0, Y - 1)], y_send.at[k, 0])
        expect(("sums in", k), settle, py[k], y_recv.at[k, 0])

    def activate(k):
        await_("sums in", k)
        total = [part[y, i] for i in range(3)]
        for d in range(Y - 1):
            total = [total[i] + py[k][d, i] for i in range(3)]
        mask = row_mask[...]
        rectified = jnp.maximum(total[1], 0.0)
        square = rectified * rectified
        grad = total[2] * mask
        act[k][y, 0] = (square * total[0] * mask).astype(BF16)
        act[k][y, 1] = (grad * square).astype(BF16)
        act[k][y, 2] = (grad * total[0] * 2.0 * rectified).astype(BF16)
        for d in range(1, Y):
            pltpu.make_async_remote_copy(
                src_ref=act[k].at[y], dst_ref=act[k].at[y], send_sem=y_send.at[k, 1],
                recv_sem=y_recv.at[k, 1], device_id=across_y(d), device_id_type=MESH).start()
        expect(("act out", k), settle, act[k].at[pl.ds(0, Y - 1)], y_send.at[k, 1])
        expect(("act in", k), settle, act[k].at[pl.ds(0, Y - 1)], y_recv.at[k, 1])

    def act_ready(k):
        await_("act in", k)

    def activation(k, i):
        return act[k][:, i].reshape(R, U)

    def give_back(u):
        a = u % 2

        def go(t):
            pltpu.make_async_remote_copy(
                src_ref=op[a].at[t], dst_ref=pr[u].at[s], send_sem=op_send.at[u], recv_sem=pr_recv.at[u],
                device_id=in_plane(t), device_id_type=MESH).start()
        each_mate(go)
        pltpu.make_async_copy(op[a].at[s], pr[u].at[s], pr_recv.at[u]).start()
        expect(("parts out", u), settle, op[a].at[pl.ds(0, S - 1)], op_send.at[u])
        expect(("parts in", u), settle, pr[u], pr_recv.at[u])

    def down(k):
        u = 2 * k
        if k:
            await_("parts out", u - 2)

        def step(columns):
            product = dot(activation(k, 0), wd[:, columns], (1, 0))
            op[0][:, :, :, columns] = product.astype(BF16).reshape(S, CAP, ROWS, columns.size)
        feature_loop(min(512, W), step)
        give_back(u)

    def back(k):
        u = 2 * k + 1
        if k:
            await_("parts out", u - 2)

        def step(columns):
            product = dot(activation(k, 1), wu[columns, :], (1, 1))
            product = product + dot(activation(k, 2), wg[columns, :], (1, 1))
            op[1][:, :, :, columns] = product.astype(BF16).reshape(S, CAP, ROWS, columns.size)
        feature_loop(min(512, W), step)
        give_back(u)

    def collected(u):
        await_("parts in", u)

    sum_rows = [S * ROWS]
    sum_at = []
    for half in range(2):
        sum_at.append([])
        for direction in range(2):
            row = []
            for count in caps[hops[half][direction]]:
                row.append(sum_rows[0])
                sum_rows[0] += count * ROWS
            sum_at[half].append(row)

    def plane_sum(u, half, direction, far, columns):
        at, count = (0, S) if far == 0 else (sum_at[half][direction][far - 1], caps[hops[half][direction]][far - 1])
        pick = sel[at:at + count * ROWS, :]
        return dot(pick, wide(pr[u], columns), (1, 0)).reshape(count, ROWS, columns.size)

    room = []
    for half in range(2):
        at, table = 0, []
        for direction in range(2):
            row, counts = [], caps[hops[half][direction]]
            for hop in range(1, len(counts) + 1):
                row.append(at)
                at += counts[max(len(counts) - hop, 1) - 1]
            table.append(row)
        room.append(table)

    def received(a, half, direction, hop, count):
        return rs[a].at[pl.ds(room[half][direction][hop - 1], count)]

    def rs_copy(u, half, direction, hop):
        a, columns = u % 2, half_of(half)
        counts = caps[hops[half][direction]]
        count = counts[len(counts) - hop]
        if hop == 1:
            source = first[a][half][direction]
        else:
            source = received(a, half, direction, hop - 1, count).at[:, :, columns]
        return pltpu.make_async_remote_copy(
            src_ref=source, dst_ref=received(a, half, direction, hop, count).at[:, :, columns],
            send_sem=rs_send.at[u, half, direction, hop - 1], recv_sem=rs_recv.at[u, half, direction, hop - 1],
            device_id=along_z(direction), device_id_type=MESH)

    def release(u, half, direction):
        if u < 2:
            pl.semaphore_signal(
                free.at[u, half, direction], inc=1, device_id=along_z(1 - direction), device_id_type=MESH)
            n = sum(key[:4] == ("free", u, half, direction) for key in pending)
            while ("free", u, half, direction, n) in pending:
                n += 1
            expect(("free", u, half, direction, n), pl.semaphore_wait, free.at[u, half, direction], 1)

    def rs_step(u, half, direction, hop):
        a = u % 2
        last = hops[half][direction]
        if hop > last:
            return
        far = last - hop + 1
        if hop == 1:
            if u >= 2:
                await_("sum out", u - 2, half, direction, 1)

            def step(columns, local):
                first[a][half][direction][:, :, local] = plane_sum(u, half, direction, far, columns).astype(BF16)
        else:
            if hop > 2:
                await_("sum out", u, half, direction, hop - 1)
                release(u, half, direction)
            await_("sum in", u, half, direction, hop - 1)
            old = caps[last][far]
            arrived = received(a, half, direction, hop - 1, old)
            fresh = rs[a].at[pl.ds(room[half][direction][hop - 2] + old, caps[last][far - 1] - old)]

            def step(columns, local):
                total = plane_sum(u, half, direction, far, columns)
                arrived[:, :, columns] = (arrived[:, :, columns].astype(F32) + total[:old]).astype(BF16)
                if caps[last][far - 1] > old:
                    fresh[:, :, columns] = total[old:].astype(BF16)
        half_loop(half, step)
        if u >= 2:
            await_(*next(key for key in pending if key[:4] == ("free", u - 2, half, direction)))
        copy = rs_copy(u, half, direction, hop)
        copy.start()
        expect(("sum out", u, half, direction, hop), copy.wait_send)
        expect(("sum in", u, half, direction, hop), copy.wait_recv)

    def rs_both(u, hop, half):
        for direction in range(2):
            rs_step(u, half, direction, hop)

    def rs_start(u):
        collected(u)
        for half in range(2):
            rs_both(u, 1, half)

    def finish(u):
        a, k = u % 2, u // 2
        for half in range(2):
            ends = []
            for direction in range(2):
                last = hops[half][direction]
                if last > 1:
                    await_("sum out", u, half, direction, last)
                    release(u, half, direction)
                await_("sum in", u, half, direction, last)
                ends.append(received(a, half, direction, last, caps[last][0]))

            def step(columns, local):
                total = plane_sum(u, half, 0, 0, columns)
                for direction in range(2):
                    arrived = ends[direction][:, :, columns].reshape(-1, columns.size)
                    total = total + dot(sort[1 - half][1 - direction][...], arrived, (0, 0)).reshape(
                        S, ROWS, columns.size)
                fin[u][:, :, columns] = total.astype(BF16)
            half_loop(half, step)
            for direction in range(2):
                release(u, half, direction)
        place = results[a].at[pl.ds(pl.multiple_of(s * SLICE + k * ROWS, ROWS), ROWS)]

        def go(t):
            pltpu.make_async_remote_copy(
                src_ref=fin[u].at[t], dst_ref=place, send_sem=fin_send.at[u], recv_sem=out_recv.at[u],
                device_id=in_plane(t), device_id_type=MESH).start()
        each_mate(go)
        pltpu.make_async_copy(fin[u].at[s], place, out_recv.at[u]).start()
        expect(("result out", u), settle, fin[u].at[pl.ds(0, S - 1)], fin_send.at[u])
        expect(("result in", u), settle, results[a].at[pl.ds(0, S * ROWS)], out_recv.at[u])

    def token_weight_grad(i, buffer, target):
        width = min(256, W)

        def step(b, carry):
            columns = pl.ds(pl.multiple_of(b * width, width), width)
            total = dot(wide(rw[0], columns), activation(0, i), (0, 0))
            total = total + dot(wide(rw[2], columns), activation(1, i), (0, 0))
            buffer[columns, :] = (total * grad_scale).astype(BF16)
            return carry
        lax.fori_loop(0, W // width, step, 0)
        copy = pltpu.make_async_copy(buffer, target, g_sem.at[i])
        copy.start()
        expect(("weights", i), copy.wait)

    def down_weight_grad(buffer, target):
        width = min(256, W)

        def step(columns):
            total = dot(activation(0, 0), wide(rw[1], columns), (0, 0))
            total = total + dot(activation(1, 0), wide(rw[3], columns), (0, 0))
            buffer[:, columns] = (total * grad_scale).astype(BF16)
        feature_loop(width, step)
        copy = pltpu.make_async_copy(buffer, target, g_sem.at[0])
        copy.start()
        expect(("weights", 0), copy.wait)

    grad_scale = 1.0 / (S * SLICE)
    weights = [pltpu.make_async_copy(wu_in, wu, w_sem.at[0]), pltpu.make_async_copy(wg_in, wg, w_sem.at[1]),
               pltpu.make_async_copy(wd_in, wd, w_sem.at[2])]
    for copy in weights:
        copy.start()

    barrier = pltpu.get_barrier_semaphore()

    def greet(device):
        pl.semaphore_signal(barrier, inc=1, device_id=device, device_id_type=MESH)
    each_mate(lambda t: greet(in_plane(t)))
    for direction in range(2):
        greet(along_z(direction))
    for d in range(1, Y):
        greet(across_y(d))
    pl.semaphore_wait(barrier, S - 1 + 2 + Y - 1)

    def sort_tables():
        for half in range(2):
            for direction in range(2):
                for r in range(caps[hops[half][direction]][0]):
                    row = lax.broadcasted_iota(jnp.int32, (ROWS, S * ROWS), 0)
                    column = lax.broadcasted_iota(jnp.int32, (ROWS, S * ROWS), 1)
                    hit = column == orders[2 * half + direction, r] * ROWS + row
                    sort[half][direction][r * ROWS:(r + 1) * ROWS, :] = jnp.where(hit, 1.0, 0.0).astype(BF16)
    def sum_table():
        def select_rows(g, carry):
            row = lax.broadcasted_iota(jnp.int32, (ROWS, R), 0)
            column = lax.broadcasted_iota(jnp.int32, (ROWS, R), 1)
            hit = (column_group[...] == sums[g]) & (lax.rem(column, ROWS) == row)
            sel[pl.ds(pl.multiple_of(g * ROWS, ROWS), ROWS), :] = jnp.where(hit, 1.0, 0.0).astype(BF16)
            return carry
        lax.fori_loop(0, sum_rows[0] // ROWS, select_rows, 0)
    def load_weights():
        for copy in weights:
            copy.wait()

    far = max(hops[0])
    steps = []

    def add(*calls):
        steps.extend(calls)

    def ring(step, u, between):
        events = [(step, u, hop, half) for hop in range(2, far + 1) for half in range(2)]
        for i in range(max(len(events), max(between, default=0)) + 1):
            add(*between.get(i, ()))
            add(*events[i:i + 1])

    add((spread, 0), (sort_tables,), (ag_start, 0), (spread, 1), (sum_table,), (load_weights,))
    ring(ag_forward, 0, {2: [(ag_start, 1), (spread, 2)]})
    ring(ag_forward, 1, {
        0: [(ag_finish, 0), (pack, 0)],
        2: [(ag_start, 2), (spread, 3)],
        5: [(rows_ready, 0), (up_and_gate, 0)]})
    ring(ag_forward, 2, {
        0: [(ag_finish, 1), (pack, 1)],
        2: [(ag_start, 3)],
        5: [(rows_ready, 1), (hidden_grad, 0), (sum_send, 0)]})
    ring(ag_forward, 3, {
        0: [(ag_finish, 2), (pack, 2)],
        1: [(activate, 0)],
        3: [(act_ready, 0), (down, 0)],
        5: [(back, 0)]})
    add((ag_finish, 3), (pack, 3), (rs_start, 0))
    ring(rs_both, 0, {
        1: [(rows_ready, 2), (up_and_gate, 1)],
        3: [(rs_start, 1)],
        5: [(rows_ready, 3), (hidden_grad, 1), (sum_send, 1)]})
    ring(rs_both, 1, {
        0: [(finish, 0)],
        1: [(activate, 1)],
        2: [(act_ready, 1), (down, 1)],
        4: [(back, 1)]})
    add((rs_start, 2))
    ring(rs_both, 2, {
        0: [(finish, 1)],
        2: [(token_weight_grad, 1, wu, gu_out)],
        4: [(rs_start, 3)],
        5: [(token_weight_grad, 2, wg, gg_out)]})
    ring(rs_both, 3, {
        0: [(finish, 2)],
        2: [(down_weight_grad, wd, gd_out)]})
    add((finish, 3))
    for call in steps:
        call[0](*call[1:])
    for wait in list(pending.values()):
        wait()


def levels(Z, S):
    far = Z // 2
    full = {far: (S,) * far, Z - 1 - far: (S,) * (Z - 1 - far)}
    if (Z, S) != (8, 8):
        return [full]
    return [{4: (8, 7, 6, 5), 3: (8, 7, 5)}, full]


def ffn(level, caps, Z, S, Y, U, held_group, slot_place, sum_orders, sort_orders, row_mask, tokens, cotangent,
        w_up, w_gate, w_down):
    group_len, W = tokens.shape
    R = S * CAP * ROWS
    quarter = R // Y
    hops = hop_counts(Z)
    start = [offsets(caps, hops[a], S) for a in range(2)]
    slots = []
    for a in range(2):
        away, rank = slot_place[a]
        first = jnp.asarray([0] + start[a][0][0] + start[a][0][1][::-1], jnp.int32)
        slots.append(jnp.sum(jnp.where(away[:, None] == jnp.arange(Z)[None, :], first[None, :], 0), axis=1) + rank)
    slots = jnp.stack(slots).astype(jnp.int32)
    sums = [sum_orders[0]]
    for a in range(2):
        for direction in range(2):
            for far, count in enumerate(caps[hops[a][direction]]):
                sums.append(sum_orders[1][a][direction][far][:count])
    sums = jnp.concatenate(sums).astype(jnp.int32)
    column_group = jnp.repeat(held_group, ROWS).reshape(1, R)

    hbm, vmem = pl.BlockSpec(memory_space=pl.ANY), pl.BlockSpec(memory_space=pltpu.VMEM)
    smem = pl.BlockSpec(memory_space=pltpu.SMEM)
    half = Z // 2
    rows = pltpu.VMEM((S, CAP, ROWS, W), BF16)
    dma = pltpu.SemaphoreType.DMA

    def groups_of(count, width=W):
        return pltpu.VMEM((count, ROWS, width), BF16)

    def counts(half, direction):
        return caps[hops[half][direction]]
    ways = [(a, direction) for a in range(2) for direction in range(2)]
    room = [sum(sum(counts(a, d)[max(len(counts(a, d)) - hop, 1) - 1] for hop in range(1, len(counts(a, d)) + 1))
                for d in range(2)) for a in range(2)]
    scratch = (
        [groups_of(start[0][1])] * 4
        + [groups_of(counts(h, d)[0], W // 2) for _ in range(2) for h, d in ways]
        + [rows] * 2 + [rows] * 4
        + [pltpu.VMEM((W, U), BF16)] * 2 + [pltpu.VMEM((U, W), BF16)]
        + [pltpu.VMEM((Y, 3, quarter, U), F32)]
        + [pltpu.VMEM((Y - 1, 3, quarter, U), F32)] * 2
        + [pltpu.VMEM((Y, 3, quarter, U), BF16)] * 2
        + [rows] * 2 + [rows] * 4
        + [groups_of(room[a]) for a in range(2)]
        + [groups_of(counts(h, d)[-1], W // 2) for _ in range(2) for h, d in ways]
        + [groups_of(S)] * 4
        + [pltpu.VMEM((sums.shape[0] * ROWS, R), BF16)]
        + [pltpu.VMEM((counts(a, d)[0] * ROWS, S * ROWS), BF16) for a, d in ways]
        + [
            dma((3,)), dma((4,)), dma((4,)), dma((4, 2, 2, half)), dma((4, 2, 2, half)), dma((4,)), dma((4,)),
            dma((2, 2)), dma((2, 2)), dma((4,)), dma((4,)), dma((4, 2, 2, half)), dma((4, 2, 2, half)), dma((4,)),
            dma((4,)), dma((3,)), pltpu.SemaphoreType.REGULAR((2, 2, 2)),
        ]
    )
    shapes = (
        jax.ShapeDtypeStruct((group_len, W), BF16), jax.ShapeDtypeStruct((group_len, W), BF16),
        jax.ShapeDtypeStruct((W, U), BF16), jax.ShapeDtypeStruct((W, U), BF16), jax.ShapeDtypeStruct((U, W), BF16),
    )
    return pl.pallas_call(
        functools.partial(kernel, Z, S, Y, W, U, caps),
        out_shape=shapes,
        in_specs=[smem] * 3 + [vmem] * 2 + [hbm] * 5,
        out_specs=[hbm] * 5,
        scratch_shapes=scratch,
        compiler_params=pltpu.CompilerParams(
            collective_id=level, has_side_effects=True, vmem_limit_bytes=63 * 1024 * 1024),
        cost_estimate=pl.CostEstimate(flops=18 * CHUNKS * R * W * U, bytes_accessed=10 * 2**20, transcendentals=0),
    )(slots, sums, sort_orders, column_group, row_mask, tokens, cotangent, w_up, w_gate, w_down)


def hand_over(*refs):
    n = (len(refs) - 1) // 3
    sems = refs[-1]
    into = [pltpu.make_async_copy(refs[i], refs[2 * n + i], sems.at[0, i]) for i in range(n)]
    onto = [pltpu.make_async_copy(refs[2 * n + i], refs[n + i], sems.at[1, i]) for i in range(n)]
    for copy in into:
        copy.start()
    for arrived, copy in zip(into, onto):
        arrived.wait()
        copy.start()
    for copy in onto:
        copy.wait()


def body(tokens, cotangent, block_masks, w_up, w_gate, w_down):
    owners, Y = lax.axis_size("seq"), lax.axis_size("ffn")
    S, Z = PLANE, owners // PLANE
    _, group_len, W = tokens.shape
    groups = block_masks.shape[0]
    U = w_up.shape[1]
    owner_blocks = U // BLK
    quarter = S * CAP * ROWS // Y
    hops = hop_counts(Z)
    my_owner = lax.axis_index("seq")
    z, s = my_owner // S, my_owner % S

    live = block_masks > 0
    need = jnp.any(live.reshape(Z, S, Z, S * owner_blocks), axis=3)
    planes = jnp.arange(Z)
    onward = (planes[None, :] - planes[:, None]) % Z
    group_in_plane = jnp.arange(S, dtype=jnp.int32)
    limits = sorted(set(hops[0]))
    keys = [(direction, limit) for direction in range(2) for limit in limits]
    distance = jnp.stack([onward if direction == 0 else (Z - onward) % Z for direction, _ in keys])
    limit_of = jnp.asarray([limit for _, limit in keys])[:, None, None]
    distance = jnp.where(distance <= limit_of, distance, 0).astype(jnp.int32)
    reach = jnp.max(jnp.where(need[None], distance[:, :, None, :], 0), axis=3)
    key = reach * S + (S - 1 - group_in_plane)
    rank = jnp.sum((key[:, :, None, :] > key[:, :, :, None]).astype(jnp.int32), axis=3)
    order = jnp.sum(
        jnp.where(rank[:, :, None, :] == group_in_plane[:, None], group_in_plane, 0), axis=3)

    mine = lax.dynamic_slice_in_dim(live, z * S * owner_blocks, S * owner_blocks, 1)
    active = jnp.any(mine.reshape(groups, S, owner_blocks), axis=2).T
    ordinal = jnp.cumsum(active.astype(jnp.int32), axis=1) - 1
    slot_ids = jnp.arange(CAP, dtype=jnp.int32)
    picked = (ordinal[:, None, :] == slot_ids[None, :, None]) & active[:, None, :]
    group_ids = jnp.arange(groups, dtype=jnp.int32)
    held = jnp.any(picked, axis=2).reshape(-1)
    picked_rows = picked.reshape(S * CAP, groups)

    def look_up(table):
        return jnp.sum(jnp.where(picked_rows, table.reshape(1, groups), 0), axis=1)
    slot_group = look_up(group_ids)
    held_group = jnp.where(held, slot_group, -1)
    away_of = jnp.where(held, (z - slot_group // S) % Z, 0)
    slot_place, sum_orders, sort_orders = [], [], []
    for a in range(2):
        ranks = [look_up(rank[keys.index((d, hops[a][d]))]) for d in range(2)]
        place = jnp.where(away_of <= hops[a][0], ranks[0], ranks[1])
        place = jnp.where(away_of == 0, jnp.where(held, slot_group % S, 0), place)
        slot_place.append((away_of, place))
        sum_orders.append([])
        for d in range(2):
            sort_orders.append(lax.dynamic_index_in_dim(order[keys.index((d, hops[a][d]))], z, 0, keepdims=False))
            row = []
            for far in range(1, hops[a][d] + 1):
                target = (z + far) % Z if d == 0 else (z + Z - far) % Z
                row.append(target * S + lax.dynamic_index_in_dim(order[keys.index((1 - d, hops[a][d]))], target, 0, keepdims=False))
            sum_orders[a].append(row)
    sort_orders = jnp.stack(sort_orders)
    own_groups = z * S + group_in_plane

    my_picked = lax.dynamic_index_in_dim(picked, s, 0, keepdims=False)
    my_columns = lax.dynamic_slice_in_dim(block_masks, my_owner * owner_blocks, owner_blocks, 1)
    block_live = jnp.sum(jnp.where(my_picked[:, :, None], my_columns[None], 0), axis=1).astype(F32)
    unit_live = jnp.repeat(block_live, BLK, axis=1)
    row_mask = jnp.broadcast_to(
        unit_live[None, :, None, :], (quarter // (CAP * ROWS), CAP, ROWS, U)).reshape(quarter, U)

    table = levels(Z, S)
    branches = [functools.partial(ffn, i, caps, Z, S, Y, U) for i, caps in enumerate(table)]
    far = max(limits)
    steps = jnp.arange(1, far + 1)[None, None, :, None]
    most = jnp.max(jnp.sum((reach[:, :, None, :] >= steps).astype(jnp.int32), axis=3), axis=1)
    allowed = [[list(caps[limit]) + [0] * (far - limit) for _, limit in keys] for caps in table]
    level = jnp.sum(jnp.any(most[None] > jnp.asarray(allowed[:-1], jnp.int32).reshape(-1, len(keys), far),
                            axis=(1, 2)).astype(jnp.int32))
    arguments = (held_group, slot_place, (own_groups, sum_orders), sort_orders, row_mask,
                 tokens.reshape(group_len, W), cotangent.reshape(group_len, W), w_up, w_gate, w_down)
    results = branches[0](*arguments) if len(table) == 1 else lax.switch(level, branches, *arguments)
    hbm = pl.BlockSpec(memory_space=pl.ANY)
    results = pl.pallas_call(
        hand_over, out_shape=tuple(jax.ShapeDtypeStruct(r.shape, r.dtype) for r in results),
        in_specs=[hbm] * len(results), out_specs=[hbm] * len(results),
        scratch_shapes=[pltpu.VMEM(r.shape, r.dtype) for r in results]
        + [pltpu.SemaphoreType.DMA((2, len(results)))],
        compiler_params=pltpu.CompilerParams(vmem_limit_bytes=32 * 1024 * 1024))(*results)
    outputs, grad_tokens, grad_up, grad_gate, grad_down = results
    return outputs[None], grad_tokens[None], grad_up, grad_gate, grad_down


def solution(mesh):
    in_specs = (
        P("seq", None, "ffn"),
        P("seq", None, "ffn"),
        P(),
        P("ffn", "seq"),
        P("ffn", "seq"),
        P("seq", "ffn"),
    )
    out_specs = (
        P("seq", None, "ffn"),
        P("seq", None, "ffn"),
        P("ffn", "seq"),
        P("ffn", "seq"),
        P("seq", "ffn"),
    )
    return jax.shard_map(body, mesh=mesh, in_specs=in_specs, out_specs=out_specs, check_vma=False)
```

```python
import functools

import jax
import jax.numpy as jnp
from jax import lax
from jax.experimental import pallas as pl
from jax.experimental.pallas import tpu as pltpu
from jax.sharding import PartitionSpec as P

BLK = 128
CAP = 3
PLANE = 8
ROWS = 16
CHUNKS = 2
MESH = pl.DeviceIdType.MESH
F32, BF16 = jnp.float32, jnp.bfloat16


def dot(left, right, dims):
    return lax.dot_general(left, right, (((dims[0],), (dims[1],)), ((), ())), preferred_element_type=F32)


def offsets(caps, hops, S):
    at, table = S, []
    for direction in range(2):
        row = []
        for count in caps[hops[direction]]:
            row.append(at)
            at += count
        table.append(row)
    return table, at


def hop_counts(Z):
    far, near = Z // 2, Z - 1 - Z // 2
    return ((far, near), (near, far))


def kernel(Z, S, Y, W, U, caps, slots, sums, orders, column_group, row_mask, tok, cot, wu_in, wg_in, wd_in,
           out, gtok, gu_out, gg_out, gd_out,
           *refs):
    refs = list(refs)

    def take(*shape):
        if not shape:
            return refs.pop(0)
        return [take(*shape[1:]) for _ in range(shape[0])]
    ag, sorted_rows, pk, rw = take(4), take(2, 2, 2), take(2), take(4)
    wu, wg, wd, part = take(4)
    py, act, op, pr, rs, first, fin = take(2), take(2), take(2), take(4), take(2), take(2, 2, 2), take(4)
    sel, sort = take(), take(2, 2)
    (w_sem, sp_send, sp_recv, ag_send, ag_recv, pk_send, rw_recv, y_send, y_recv,
     op_send, pr_recv, rs_send, rs_recv, fin_send, out_recv, g_sem, free) = take(17)
    sources, results = (tok, cot), (out, gtok)
    R = S * CAP * ROWS
    SLICE = CHUNKS * ROWS
    seq, y = lax.axis_index("seq"), lax.axis_index("ffn")
    z, s = seq // S, seq % S
    up_z, down_z = lax.rem(z + 1, Z), lax.rem(z + Z - 1, Z)
    toward = (up_z, down_z)
    hops = hop_counts(Z)
    blocks = [offsets(caps, hops[half], S)[0] for half in range(2)]

    def mate(d):
        return lax.rem(s + d, S)

    def in_plane(t):
        return (z * S + t, y)

    def along_z(direction):
        return (toward[direction] * S + s, y)

    def across_y(d):
        return (seq, lax.rem(y + d, Y))

    def each_mate(fn):
        def step(d, carry):
            fn(mate(d))
            return carry
        lax.fori_loop(1, S, step, 0)

    pending = {}

    def settle(ref, sem):
        pltpu.make_async_copy(ref, ref, sem).wait()

    def expect(key, *wait):
        pending[key] = functools.partial(*wait)

    def await_(*key):
        pending.pop(key)()

    def spread(u):
        source, k = sources[u % 2], u // 2

        def piece(t):
            return source.at[pl.ds(pl.multiple_of(t * SLICE + k * ROWS, ROWS), ROWS)]

        def go(t):
            pltpu.make_async_remote_copy(
                src_ref=piece(t), dst_ref=ag[u].at[s], send_sem=sp_send.at[u], recv_sem=sp_recv.at[u],
                device_id=in_plane(t), device_id_type=MESH).start()
        each_mate(go)
        pltpu.make_async_copy(piece(s), ag[u].at[s], sp_recv.at[u]).start()
        expect(("spread out", u), settle, source.at[pl.ds(0, (S - 1) * ROWS)], sp_send.at[u])
        expect(("spread in", u), settle, ag[u].at[pl.ds(0, S)], sp_recv.at[u])

    def arrivals(half, direction, hop, count):
        return pl.ds(blocks[half][direction][hop - 1], count)

    def ag_copy(u, half, direction, hop):
        columns = half_of(half)
        count = caps[hops[half][direction]][hop - 1]
        if hop == 1:
            source = sorted_rows[u % 2][half][direction]
        else:
            source = ag[u].at[arrivals(half, direction, hop - 1, count), :, columns]
        return pltpu.make_async_remote_copy(
            src_ref=source, dst_ref=ag[u].at[arrivals(half, direction, hop, count), :, columns],
            send_sem=ag_send.at[u, half, direction, hop - 1], recv_sem=ag_recv.at[u, half, direction, hop - 1],
            device_id=along_z(direction), device_id_type=MESH)

    def ag_start(u):
        a = u % 2
        await_("spread in", u)
        for half in range(2):
            for direction in range(2):
                target = sorted_rows[a][half][direction]
                if u >= 2:
                    await_("gather out", u - 2, half, direction, 1)

                def step(columns, local):
                    own = ag[u][0:S, :, columns].reshape(S * ROWS, columns.size)
                    moved = dot(sort[half][direction][...], own, (1, 0)).astype(BF16)
                    target[:, :, local] = moved.reshape(target.shape[0], ROWS, columns.size)
                half_loop(half, step)
                ag_send_on(u, half, direction, 1)

    def ag_send_on(u, half, direction, hop):
        copy = ag_copy(u, half, direction, hop)
        copy.start()
        expect(("gather out", u, half, direction, hop), copy.wait_send)
        expect(("gather in", u, half, direction, hop), copy.wait_recv)

    def ag_forward(u, hop, half):
        for direction in range(2):
            if hop <= hops[half][direction]:
                await_("gather in", u, half, direction, hop - 1)
                ag_send_on(u, half, direction, hop)

    def ag_finish(u):
        for half in range(2):
            for direction in range(2):
                await_("gather in", u, half, direction, hops[half][direction])

    def pack(u):
        a = u % 2
        if u >= 2:
            await_("rows out", u - 2)

        def go(t):
            for j in range(CAP):
                for half in range(2):
                    columns = half_of(half)
                    pk[a][t, j, :, columns] = ag[u][slots[half, t * CAP + j], :, columns]
            pltpu.make_async_remote_copy(
                src_ref=pk[a].at[t], dst_ref=rw[u].at[s], send_sem=pk_send.at[u], recv_sem=rw_recv.at[u],
                device_id=in_plane(t), device_id_type=MESH).start()
        each_mate(go)
        for j in range(CAP):
            for half in range(2):
                columns = half_of(half)
                rw[u][s, j, :, columns] = ag[u][slots[half, s * CAP + j], :, columns]
        expect(("rows out", u), settle, pk[a].at[pl.ds(0, S - 1)], pk_send.at[u])
        expect(("rows in", u), settle, rw[u].at[pl.ds(0, S - 1)], rw_recv.at[u])

    def rows_ready(u):
        await_("rows in", u)

    def feature_loop(width, fn):
        def step(b, carry):
            fn(pl.ds(pl.multiple_of(b * width, width), width))
            return carry
        lax.fori_loop(0, W // width, step, 0)

    HALF = W // 2
    piece_width = min(512, HALF)

    def half_of(half):
        return pl.ds(half * HALF, HALF)

    def half_loop(half, fn):
        def step(b, carry):
            local = pl.multiple_of(b * piece_width, piece_width)
            fn(pl.ds(pl.multiple_of(half * HALF + local, piece_width), piece_width), pl.ds(local, piece_width))
            return carry
        lax.fori_loop(0, HALF // piece_width, step, 0)

    def wide(ref, columns):
        return ref[:, :, :, columns].reshape(R, columns.size)

    def split(rows):
        return rows.reshape(Y, R // Y, U)

    def up_and_gate(k):
        if k:
            await_("sums out", k - 1)
        part[...] = jnp.zeros_like(part)

        def step(columns):
            x = wide(rw[2 * k], columns)
            part[:, 0] += split(dot(x, wu[columns, :], (1, 0)))
            part[:, 1] += split(dot(x, wg[columns, :], (1, 0)))
        feature_loop(min(512, W), step)

    def hidden_grad(k):
        def step(columns):
            x = wide(rw[2 * k + 1], columns)
            part[:, 2] += split(dot(x, wd[:, columns], (1, 1)))
        feature_loop(min(512, W), step)

    def sum_send(k):
        for d in range(1, Y):
            pltpu.make_async_remote_copy(
                src_ref=part.at[lax.rem(y + d, Y)], dst_ref=py[k].at[d - 1], send_sem=y_send.at[k, 0],
                recv_sem=y_recv.at[k, 0], device_id=across_y(d), device_id_type=MESH).start()
        expect(("sums out", k), settle, part.at[pl.ds(0, Y - 1)], y_send.at[k, 0])
        expect(("sums in", k), settle, py[k], y_recv.at[k, 0])

    def activate(k):
        await_("sums in", k)
        total = [part[y, i] for i in range(3)]
        for d in range(Y - 1):
            total = [total[i] + py[k][d, i] for i in range(3)]
        mask = row_mask[...]
        rectified = jnp.maximum(total[1], 0.0)
        square = rectified * rectified
        grad = total[2] * mask
        act[k][y, 0] = (square * total[0] * mask).astype(BF16)
        act[k][y, 1] = (grad * square).astype(BF16)
        act[k][y, 2] = (grad * total[0] * 2.0 * rectified).astype(BF16)
        for d in range(1, Y):
            pltpu.make_async_remote_copy(
                src_ref=act[k].at[y], dst_ref=act[k].at[y], send_sem=y_send.at[k, 1],
                recv_sem=y_recv.at[k, 1], device_id=across_y(d), device_id_type=MESH).start()
        expect(("act out", k), settle, act[k].at[pl.ds(0, Y - 1)], y_send.at[k, 1])
        expect(("act in", k), settle, act[k].at[pl.ds(0, Y - 1)], y_recv.at[k, 1])

    def act_ready(k):
        await_("act in", k)

    def activation(k, i):
        return act[k][:, i].reshape(R, U)

    def give_back(u):
        a = u % 2

        def go(t):
            pltpu.make_async_remote_copy(
                src_ref=op[a].at[t], dst_ref=pr[u].at[s], send_sem=op_send.at[u], recv_sem=pr_recv.at[u],
                device_id=in_plane(t), device_id_type=MESH).start()
        each_mate(go)
        pltpu.make_async_copy(op[a].at[s], pr[u].at[s], pr_recv.at[u]).start()
        expect(("parts out", u), settle, op[a].at[pl.ds(0, S - 1)], op_send.at[u])
        expect(("parts in", u), settle, pr[u], pr_recv.at[u])

    def down(k):
        u = 2 * k
        if k:
            await_("parts out", u - 2)

        def step(columns):
            product = dot(activation(k, 0), wd[:, columns], (1, 0))
            op[0][:, :, :, columns] = product.astype(BF16).reshape(S, CAP, ROWS, columns.size)
        feature_loop(min(512, W), step)
        give_back(u)

    def back(k):
        u = 2 * k + 1
        if k:
            await_("parts out", u - 2)

        def step(columns):
            product = dot(activation(k, 1), wu[columns, :], (1, 1))
            product = product + dot(activation(k, 2), wg[columns, :], (1, 1))
            op[1][:, :, :, columns] = product.astype(BF16).reshape(S, CAP, ROWS, columns.size)
        feature_loop(min(512, W), step)
        give_back(u)

    def collected(u):
        await_("parts in", u)

    sum_rows = [S * ROWS]
    sum_at = []
    for half in range(2):
        sum_at.append([])
        for direction in range(2):
            row = []
            for count in caps[hops[half][direction]]:
                row.append(sum_rows[0])
                sum_rows[0] += count * ROWS
            sum_at[half].append(row)

    def plane_sum(u, half, direction, far, columns):
        at, count = (0, S) if far == 0 else (sum_at[half][direction][far - 1], caps[hops[half][direction]][far - 1])
        pick = sel[at:at + count * ROWS, :]
        return dot(pick, wide(pr[u], columns), (1, 0)).reshape(count, ROWS, columns.size)

    room = []
    for half in range(2):
        at, table = 0, []
        for direction in range(2):
            row, counts = [], caps[hops[half][direction]]
            for hop in range(1, len(counts) + 1):
                row.append(at)
                at += counts[max(len(counts) - hop, 1) - 1]
            table.append(row)
        room.append(table)

    def received(a, half, direction, hop, count):
        return rs[a].at[pl.ds(room[half][direction][hop - 1], count)]

    def rs_copy(u, half, direction, hop):
        a, columns = u % 2, half_of(half)
        counts = caps[hops[half][direction]]
        count = counts[len(counts) - hop]
        if hop == 1:
            source = first[a][half][direction]
        else:
            source = received(a, half, direction, hop - 1, count).at[:, :, columns]
        return pltpu.make_async_remote_copy(
            src_ref=source, dst_ref=received(a, half, direction, hop, count).at[:, :, columns],
            send_sem=rs_send.at[u, half, direction, hop - 1], recv_sem=rs_recv.at[u, half, direction, hop - 1],
            device_id=along_z(direction), device_id_type=MESH)

    def release(u, half, direction):
        if u < 2:
            pl.semaphore_signal(
                free.at[u, half, direction], inc=1, device_id=along_z(1 - direction), device_id_type=MESH)
            n = sum(key[:4] == ("free", u, half, direction) for key in pending)
            while ("free", u, half, direction, n) in pending:
                n += 1
            expect(("free", u, half, direction, n), pl.semaphore_wait, free.at[u, half, direction], 1)

    def rs_step(u, half, direction, hop):
        a = u % 2
        last = hops[half][direction]
        if hop > last:
            return
        far = last - hop + 1
        if hop == 1:
            if u >= 2:
                await_("sum out", u - 2, half, direction, 1)

            def step(columns, local):
                first[a][half][direction][:, :, local] = plane_sum(u, half, direction, far, columns).astype(BF16)
        else:
            if hop > 2:
                await_("sum out", u, half, direction, hop - 1)
                release(u, half, direction)
            await_("sum in", u, half, direction, hop - 1)
            old = caps[last][far]
            arrived = received(a, half, direction, hop - 1, old)
            fresh = rs[a].at[pl.ds(room[half][direction][hop - 2] + old, caps[last][far - 1] - old)]

            def step(columns, local):
                total = plane_sum(u, half, direction, far, columns)
                arrived[:, :, columns] = (arrived[:, :, columns].astype(F32) + total[:old]).astype(BF16)
                if caps[last][far - 1] > old:
                    fresh[:, :, columns] = total[old:].astype(BF16)
        half_loop(half, step)
        if u >= 2:
            await_(*next(key for key in pending if key[:4] == ("free", u - 2, half, direction)))
        copy = rs_copy(u, half, direction, hop)
        copy.start()
        expect(("sum out", u, half, direction, hop), copy.wait_send)
        expect(("sum in", u, half, direction, hop), copy.wait_recv)

    def rs_both(u, hop, half):
        for direction in range(2):
            rs_step(u, half, direction, hop)

    def rs_start(u):
        collected(u)
        for half in range(2):
            rs_both(u, 1, half)

    def finish(u):
        a, k = u % 2, u // 2
        for half in range(2):
            ends = []
            for direction in range(2):
                last = hops[half][direction]
                if last > 1:
                    await_("sum out", u, half, direction, last)
                    release(u, half, direction)
                await_("sum in", u, half, direction, last)
                ends.append(received(a, half, direction, last, caps[last][0]))

            def step(columns, local):
                total = plane_sum(u, half, 0, 0, columns)
                for direction in range(2):
                    arrived = ends[direction][:, :, columns].reshape(-1, columns.size)
                    total = total + dot(sort[1 - half][1 - direction][...], arrived, (0, 0)).reshape(
                        S, ROWS, columns.size)
                fin[u][:, :, columns] = total.astype(BF16)
            half_loop(half, step)
            for direction in range(2):
                release(u, half, direction)
        place = results[a].at[pl.ds(pl.multiple_of(s * SLICE + k * ROWS, ROWS), ROWS)]

        def go(t):
            pltpu.make_async_remote_copy(
                src_ref=fin[u].at[t], dst_ref=place, send_sem=fin_send.at[u], recv_sem=out_recv.at[u],
                device_id=in_plane(t), device_id_type=MESH).start()
        each_mate(go)
        pltpu.make_async_copy(fin[u].at[s], place, out_recv.at[u]).start()
        expect(("result out", u), settle, fin[u].at[pl.ds(0, S - 1)], fin_send.at[u])
        expect(("result in", u), settle, results[a].at[pl.ds(0, S * ROWS)], out_recv.at[u])

    def token_weight_grad(i, buffer, target):
        width = min(256, W)

        def step(b, carry):
            columns = pl.ds(pl.multiple_of(b * width, width), width)
            total = dot(wide(rw[0], columns), activation(0, i), (0, 0))
            total = total + dot(wide(rw[2], columns), activation(1, i), (0, 0))
            buffer[columns, :] = (total * grad_scale).astype(BF16)
            return carry
        lax.fori_loop(0, W // width, step, 0)
        copy = pltpu.make_async_copy(buffer, target, g_sem.at[i])
        copy.start()
        expect(("weights", i), copy.wait)

    def down_weight_grad(buffer, target):
        width = min(256, W)

        def step(columns):
            total = dot(activation(0, 0), wide(rw[1], columns), (0, 0))
            total = total + dot(activation(1, 0), wide(rw[3], columns), (0, 0))
            buffer[:, columns] = (total * grad_scale).astype(BF16)
        feature_loop(width, step)
        copy = pltpu.make_async_copy(buffer, target, g_sem.at[0])
        copy.start()
        expect(("weights", 0), copy.wait)

    grad_scale = 1.0 / (S * SLICE)
    weights = [pltpu.make_async_copy(wu_in, wu, w_sem.at[0]), pltpu.make_async_copy(wg_in, wg, w_sem.at[1]),
               pltpu.make_async_copy(wd_in, wd, w_sem.at[2])]
    for copy in weights:
        copy.start()

    barrier = pltpu.get_barrier_semaphore()

    def greet(device):
        pl.semaphore_signal(barrier, inc=1, device_id=device, device_id_type=MESH)
    each_mate(lambda t: greet(in_plane(t)))
    for direction in range(2):
        greet(along_z(direction))
    for d in range(1, Y):
        greet(across_y(d))
    pl.semaphore_wait(barrier, S - 1 + 2 + Y - 1)

    def sort_tables():
        for half in range(2):
            for direction in range(2):
                for r in range(caps[hops[half][direction]][0]):
                    row = lax.broadcasted_iota(jnp.int32, (ROWS, S * ROWS), 0)
                    column = lax.broadcasted_iota(jnp.int32, (ROWS, S * ROWS), 1)
                    hit = column == orders[2 * half + direction, r] * ROWS + row
                    sort[half][direction][r * ROWS:(r + 1) * ROWS, :] = jnp.where(hit, 1.0, 0.0).astype(BF16)
    def sum_table():
        def select_rows(g, carry):
            row = lax.broadcasted_iota(jnp.int32, (ROWS, R), 0)
            column = lax.broadcasted_iota(jnp.int32, (ROWS, R), 1)
            hit = (column_group[...] == sums[g]) & (lax.rem(column, ROWS) == row)
            sel[pl.ds(pl.multiple_of(g * ROWS, ROWS), ROWS), :] = jnp.where(hit, 1.0, 0.0).astype(BF16)
            return carry
        lax.fori_loop(0, sum_rows[0] // ROWS, select_rows, 0)
    def load_weights():
        for copy in weights:
            copy.wait()

    far = max(hops[0])
    steps = []

    def add(*calls):
        steps.extend(calls)

    def ring(step, u, between):
        events = [(step, u, hop, half) for hop in range(2, far + 1) for half in range(2)]
        for i in range(max(len(events), max(between, default=0)) + 1):
            add(*between.get(i, ()))
            add(*events[i:i + 1])

    add((spread, 0), (sort_tables,), (ag_start, 0), (spread, 1), (sum_table,), (load_weights,))
    ring(ag_forward, 0, {2: [(ag_start, 1), (spread, 2)]})
    ring(ag_forward, 1, {
        0: [(ag_finish, 0), (pack, 0)],
        2: [(ag_start, 2), (spread, 3)],
        5: [(rows_ready, 0), (up_and_gate, 0)]})
    ring(ag_forward, 2, {
        0: [(ag_finish, 1), (pack, 1)],
        2: [(ag_start, 3)],
        5: [(rows_ready, 1), (hidden_grad, 0), (sum_send, 0)]})
    ring(ag_forward, 3, {
        0: [(ag_finish, 2), (pack, 2)],
        1: [(activate, 0)],
        3: [(act_ready, 0), (down, 0)],
        5: [(back, 0)]})
    add((ag_finish, 3), (pack, 3), (rs_start, 0))
    ring(rs_both, 0, {
        1: [(rows_ready, 2), (up_and_gate, 1)],
        3: [(rs_start, 1)],
        5: [(rows_ready, 3), (hidden_grad, 1), (sum_send, 1)]})
    ring(rs_both, 1, {
        0: [(finish, 0)],
        1: [(activate, 1)],
        2: [(act_ready, 1), (down, 1)],
        4: [(back, 1)]})
    add((rs_start, 2))
    ring(rs_both, 2, {
        0: [(finish, 1)],
        2: [(token_weight_grad, 1, wu, gu_out)],
        4: [(rs_start, 3)],
        5: [(token_weight_grad, 2, wg, gg_out)]})
    ring(rs_both, 3, {
        0: [(finish, 2)],
        2: [(down_weight_grad, wd, gd_out)]})
    add((finish, 3))
    for call in steps:
        call[0](*call[1:])
    for wait in list(pending.values()):
        wait()


def levels(Z, S):
    far = Z // 2
    full = {far: (S,) * far, Z - 1 - far: (S,) * (Z - 1 - far)}
    if (Z, S) != (8, 8):
        return [full]
    return [{4: (8, 7, 6, 4), 3: (7, 6, 4)}, {4: (8, 7, 6, 5), 3: (8, 7, 5)}, full]


def ffn(level, caps, Z, S, Y, U, held_group, slot_place, sum_orders, sort_orders, row_mask, tokens, cotangent,
        w_up, w_gate, w_down):
    group_len, W = tokens.shape
    R = S * CAP * ROWS
    quarter = R // Y
    hops = hop_counts(Z)
    start = [offsets(caps, hops[a], S) for a in range(2)]
    slots = []
    for a in range(2):
        away, rank = slot_place[a]
        first = jnp.asarray([0] + start[a][0][0] + start[a][0][1][::-1], jnp.int32)
        slots.append(jnp.sum(jnp.where(away[:, None] == jnp.arange(Z)[None, :], first[None, :], 0), axis=1) + rank)
    slots = jnp.stack(slots).astype(jnp.int32)
    sums = [sum_orders[0]]
    for a in range(2):
        for direction in range(2):
            for far, count in enumerate(caps[hops[a][direction]]):
                sums.append(sum_orders[1][a][direction][far][:count])
    sums = jnp.concatenate(sums).astype(jnp.int32)
    column_group = jnp.repeat(held_group, ROWS).reshape(1, R)

    hbm, vmem = pl.BlockSpec(memory_space=pl.ANY), pl.BlockSpec(memory_space=pltpu.VMEM)
    smem = pl.BlockSpec(memory_space=pltpu.SMEM)
    half = Z // 2
    rows = pltpu.VMEM((S, CAP, ROWS, W), BF16)
    dma = pltpu.SemaphoreType.DMA

    def groups_of(count, width=W):
        return pltpu.VMEM((count, ROWS, width), BF16)

    def counts(half, direction):
        return caps[hops[half][direction]]
    ways = [(a, direction) for a in range(2) for direction in range(2)]
    room = [sum(sum(counts(a, d)[max(len(counts(a, d)) - hop, 1) - 1] for hop in range(1, len(counts(a, d)) + 1))
                for d in range(2)) for a in range(2)]
    scratch = (
        [groups_of(start[0][1])] * 4
        + [groups_of(counts(h, d)[0], W // 2) for _ in range(2) for h, d in ways]
        + [rows] * 2 + [rows] * 4
        + [pltpu.VMEM((W, U), BF16)] * 2 + [pltpu.VMEM((U, W), BF16)]
        + [pltpu.VMEM((Y, 3, quarter, U), F32)]
        + [pltpu.VMEM((Y - 1, 3, quarter, U), F32)] * 2
        + [pltpu.VMEM((Y, 3, quarter, U), BF16)] * 2
        + [rows] * 2 + [rows] * 4
        + [groups_of(room[a]) for a in range(2)]
        + [groups_of(counts(h, d)[-1], W // 2) for _ in range(2) for h, d in ways]
        + [groups_of(S)] * 4
        + [pltpu.VMEM((sums.shape[0] * ROWS, R), BF16)]
        + [pltpu.VMEM((counts(a, d)[0] * ROWS, S * ROWS), BF16) for a, d in ways]
        + [
            dma((3,)), dma((4,)), dma((4,)), dma((4, 2, 2, half)), dma((4, 2, 2, half)), dma((4,)), dma((4,)),
            dma((2, 2)), dma((2, 2)), dma((4,)), dma((4,)), dma((4, 2, 2, half)), dma((4, 2, 2, half)), dma((4,)),
            dma((4,)), dma((3,)), pltpu.SemaphoreType.REGULAR((2, 2, 2)),
        ]
    )
    shapes = (
        jax.ShapeDtypeStruct((group_len, W), BF16), jax.ShapeDtypeStruct((group_len, W), BF16),
        jax.ShapeDtypeStruct((W, U), BF16), jax.ShapeDtypeStruct((W, U), BF16), jax.ShapeDtypeStruct((U, W), BF16),
    )
    return pl.pallas_call(
        functools.partial(kernel, Z, S, Y, W, U, caps),
        out_shape=shapes,
        in_specs=[smem] * 3 + [vmem] * 2 + [hbm] * 5,
        out_specs=[hbm] * 5,
        scratch_shapes=scratch,
        compiler_params=pltpu.CompilerParams(
            collective_id=level, has_side_effects=True, vmem_limit_bytes=63 * 1024 * 1024),
        cost_estimate=pl.CostEstimate(flops=18 * CHUNKS * R * W * U, bytes_accessed=10 * 2**20, transcendentals=0),
    )(slots, sums, sort_orders, column_group, row_mask, tokens, cotangent, w_up, w_gate, w_down)


def hand_over(*refs):
    n = (len(refs) - 1) // 3
    sems = refs[-1]
    into = [pltpu.make_async_copy(refs[i], refs[2 * n + i], sems.at[0, i]) for i in range(n)]
    onto = [pltpu.make_async_copy(refs[2 * n + i], refs[n + i], sems.at[1, i]) for i in range(n)]
    for copy in into:
        copy.start()
    for arrived, copy in zip(into, onto):
        arrived.wait()
        copy.start()
    for copy in onto:
        copy.wait()


def body(tokens, cotangent, block_masks, w_up, w_gate, w_down):
    owners, Y = lax.axis_size("seq"), lax.axis_size("ffn")
    S, Z = PLANE, owners // PLANE
    _, group_len, W = tokens.shape
    groups = block_masks.shape[0]
    U = w_up.shape[1]
    owner_blocks = U // BLK
    quarter = S * CAP * ROWS // Y
    hops = hop_counts(Z)
    my_owner = lax.axis_index("seq")
    z, s = my_owner // S, my_owner % S

    live = block_masks > 0
    need = jnp.any(live.reshape(Z, S, Z, S * owner_blocks), axis=3)
    planes = jnp.arange(Z)
    onward = (planes[None, :] - planes[:, None]) % Z
    group_in_plane = jnp.arange(S, dtype=jnp.int32)
    limits = sorted(set(hops[0]))
    keys = [(direction, limit) for direction in range(2) for limit in limits]
    distance = jnp.stack([onward if direction == 0 else (Z - onward) % Z for direction, _ in keys])
    limit_of = jnp.asarray([limit for _, limit in keys])[:, None, None]
    distance = jnp.where(distance <= limit_of, distance, 0).astype(jnp.int32)
    reach = jnp.max(jnp.where(need[None], distance[:, :, None, :], 0), axis=3)
    key = reach * S + (S - 1 - group_in_plane)
    rank = jnp.sum((key[:, :, None, :] > key[:, :, :, None]).astype(jnp.int32), axis=3)
    order = jnp.sum(
        jnp.where(rank[:, :, None, :] == group_in_plane[:, None], group_in_plane, 0), axis=3)

    mine = lax.dynamic_slice_in_dim(live, z * S * owner_blocks, S * owner_blocks, 1)
    active = jnp.any(mine.reshape(groups, S, owner_blocks), axis=2).T
    ordinal = jnp.cumsum(active.astype(jnp.int32), axis=1) - 1
    slot_ids = jnp.arange(CAP, dtype=jnp.int32)
    picked = (ordinal[:, None, :] == slot_ids[None, :, None]) & active[:, None, :]
    group_ids = jnp.arange(groups, dtype=jnp.int32)
    held = jnp.any(picked, axis=2).reshape(-1)
    picked_rows = picked.reshape(S * CAP, groups)

    def look_up(table):
        return jnp.sum(jnp.where(picked_rows, table.reshape(1, groups), 0), axis=1)
    slot_group = look_up(group_ids)
    held_group = jnp.where(held, slot_group, -1)
    away_of = jnp.where(held, (z - slot_group // S) % Z, 0)
    slot_place, sum_orders, sort_orders = [], [], []
    for a in range(2):
        ranks = [look_up(rank[keys.index((d, hops[a][d]))]) for d in range(2)]
        place = jnp.where(away_of <= hops[a][0], ranks[0], ranks[1])
        place = jnp.where(away_of == 0, jnp.where(held, slot_group % S, 0), place)
        slot_place.append((away_of, place))
        sum_orders.append([])
        for d in range(2):
            sort_orders.append(lax.dynamic_index_in_dim(order[keys.index((d, hops[a][d]))], z, 0, keepdims=False))
            row = []
            for far in range(1, hops[a][d] + 1):
                target = (z + far) % Z if d == 0 else (z + Z - far) % Z
                row.append(target * S + lax.dynamic_index_in_dim(order[keys.index((1 - d, hops[a][d]))], target, 0, keepdims=False))
            sum_orders[a].append(row)
    sort_orders = jnp.stack(sort_orders)
    own_groups = z * S + group_in_plane

    my_picked = lax.dynamic_index_in_dim(picked, s, 0, keepdims=False)
    my_columns = lax.dynamic_slice_in_dim(block_masks, my_owner * owner_blocks, owner_blocks, 1)
    block_live = jnp.sum(jnp.where(my_picked[:, :, None], my_columns[None], 0), axis=1).astype(F32)
    unit_live = jnp.repeat(block_live, BLK, axis=1)
    row_mask = jnp.broadcast_to(
        unit_live[None, :, None, :], (quarter // (CAP * ROWS), CAP, ROWS, U)).reshape(quarter, U)

    table = levels(Z, S)
    branches = [functools.partial(ffn, i, caps, Z, S, Y, U) for i, caps in enumerate(table)]
    far = max(limits)
    steps = jnp.arange(1, far + 1)[None, None, :, None]
    most = jnp.max(jnp.sum((reach[:, :, None, :] >= steps).astype(jnp.int32), axis=3), axis=1)
    allowed = [[list(caps[limit]) + [0] * (far - limit) for _, limit in keys] for caps in table]
    level = jnp.sum(jnp.any(most[None] > jnp.asarray(allowed[:-1], jnp.int32).reshape(-1, len(keys), far),
                            axis=(1, 2)).astype(jnp.int32))
    arguments = (held_group, slot_place, (own_groups, sum_orders), sort_orders, row_mask,
                 tokens.reshape(group_len, W), cotangent.reshape(group_len, W), w_up, w_gate, w_down)
    results = branches[0](*arguments) if len(table) == 1 else lax.switch(level, branches, *arguments)
    hbm = pl.BlockSpec(memory_space=pl.ANY)
    results = pl.pallas_call(
        hand_over, out_shape=tuple(jax.ShapeDtypeStruct(r.shape, r.dtype) for r in results),
        in_specs=[hbm] * len(results), out_specs=[hbm] * len(results),
        scratch_shapes=[pltpu.VMEM(r.shape, r.dtype) for r in results]
        + [pltpu.SemaphoreType.DMA((2, len(results)))],
        compiler_params=pltpu.CompilerParams(vmem_limit_bytes=32 * 1024 * 1024))(*results)
    outputs, grad_tokens, grad_up, grad_gate, grad_down = results
    return outputs[None], grad_tokens[None], grad_up, grad_gate, grad_down


def solution(mesh):
    in_specs = (
        P("seq", None, "ffn"),
        P("seq", None, "ffn"),
        P(),
        P("ffn", "seq"),
        P("ffn", "seq"),
        P("seq", "ffn"),
    )
    out_specs = (
        P("seq", None, "ffn"),
        P("seq", None, "ffn"),
        P("ffn", "seq"),
        P("ffn", "seq"),
        P("seq", "ffn"),
    )
    return jax.shard_map(body, mesh=mesh, in_specs=in_specs, out_specs=out_specs, check_vma=False)
```
